256 devices in a mesh: dp: 32 (over z, x), tensor: 8 (over y, core).
Axes of the slice: x: 4, y: 4, z: 8, core: 2. Of those that a mesh axis runs over, the one named last changes fastest.
Arguments:
- prompt_states: bfloat16 [128, 256, 5120], P('dp', None, 'tensor'), may hold values from -18 to 18
- prompt_lengths: int32 [128], replicated, may hold values from 1 to 256, 16384 in all
- decode_states: bfloat16 [2048, 4, 5120], P('dp', None, 'tensor'), may hold values from -18 to 18
- sample_owner: int32 [2048, 1], P('dp'), may hold values from 0 to 31; in each aligned block of 64 rows (0 to 63, 64 to 127, ...) at most 4 rows name the same one
- sample_local: int32 [2048], P('dp'), may hold values from 0 to 3
- norm_gain: float32 [5120], P('tensor'), may hold values from 0.5 to 2
- kv_weight: bfloat16 [5120, 8, 256], P(None, 'tensor'), may hold values from -1 to 1
- q_weight: bfloat16 [5120, 8, 384], P(None, 'tensor'), may hold values from -1 to 1
- output_weight: bfloat16 [8, 384, 5120], P('tensor'), may hold values from -0.3125 to 0.3125
Outputs:
- layer_out: bfloat16 [2048, 4, 5120], P('dp', None, 'tensor')
The draws below stay inside these ranges and needn't reach their ends.
Inputs may be any that keep to these rules, and one draw needn't show every extreme that they name: `prompt_lengths`: the longest prompt has exactly 256 live positions. `sample_owner`: among the 64 samples of one dp index at most 4 name the same owner; in some dp index one owner is named exactly 4 times.
All inputs are finite; a program needn't handle non-finite values.
Results may differ from the reference program's by a relative error of at most 0.03.
Values may be sent and summed in bfloat16 or wider, within the bound.
A program may use at most 128 MiB of HBM per device.

```python
import math
import jax
import jax.numpy as jnp
import numpy as np
from jax import lax

MODEL_WIDTH = 5120
KEY_VALUE_HEADS = 8
HEAD_WIDTH = 128
QUERIES_PER_KEY = 3
P_DEV = 4
LP = 256
S_DEV = 64
STEPS = 4
PROMPTS = 128
SAMPLES = 2048
OWNERS = 32
CAP = 4
N_DP = 32


def shared_pattern(key):
    feature_sign = jnp.where(jax.random.bernoulli(jax.random.fold_in(key, 101), 0.5, (MODEL_WIDTH,)), 1.0, -1.0).astype(jnp.float32)
    column_polarity = jnp.where(jax.random.bernoulli(jax.random.fold_in(key, 102), 0.5, (KEY_VALUE_HEADS, HEAD_WIDTH)), 1.0, -1.0).astype(jnp.float32)
    head_sequence = jax.random.permutation(jax.random.fold_in(key, 103), KEY_VALUE_HEADS)
    chosen = jnp.where(head_sequence < 2, 1.0, 0.0).astype(jnp.float32)
    return (feature_sign, column_polarity, chosen)


def drawn_columns(feature_sign, column_polarity, chosen):
    strength = 20.0 / HEAD_WIDTH ** 0.25 / MODEL_WIDTH
    return strength * feature_sign[:, None, None] * (column_polarity * chosen[:, None])[None, :, :]


def plant_rows(random_part, aligned, strength, feature_sign):
    rising = 0.6 * 3.0 ** (jnp.arange(MODEL_WIDTH, dtype=jnp.float32) / (MODEL_WIDTH - 1))
    return (rising * (random_part + (aligned * strength)[..., None] * feature_sign)).astype(jnp.bfloat16)


def draw_prompt_states(key, part):
    feature_sign, column_polarity, chosen = shared_pattern(key)
    key = jax.random.fold_in(key, 2)
    complete_shape = (PROMPTS, LP, MODEL_WIDTH)
    random_part = jax.random.truncated_normal(jax.random.fold_in(key, 1), -6.0, 6.0, complete_shape, jnp.float32)
    aligned = jax.random.bernoulli(jax.random.fold_in(key, 2), 2.0 / LP, (PROMPTS, LP)).astype(jnp.float32)
    strength = jax.random.uniform(jax.random.fold_in(key, 3), (PROMPTS, LP), jnp.float32, 1.0, 4.0)
    return plant_rows(random_part, aligned, strength, feature_sign)


def draw_decode_states(key, part):
    feature_sign, column_polarity, chosen = shared_pattern(key)
    key = jax.random.fold_in(key, 3)
    complete_shape = (SAMPLES, STEPS, MODEL_WIDTH)
    random_part = jax.random.truncated_normal(jax.random.fold_in(key, 1), -6.0, 6.0, complete_shape, jnp.float32)
    aligned = jax.random.bernoulli(jax.random.fold_in(key, 2), 0.125, (SAMPLES, STEPS)).astype(jnp.float32)
    strength = jax.random.uniform(jax.random.fold_in(key, 3), (SAMPLES, STEPS), jnp.float32, 1.0, 4.0)
    return plant_rows(random_part, aligned, strength, feature_sign)


def draw_kv_weight(key, part):
    feature_sign, column_polarity, chosen = shared_pattern(key)
    key = jax.random.fold_in(key, 4)
    complete_shape = (MODEL_WIDTH, KEY_VALUE_HEADS, 2 * HEAD_WIDTH)
    random_part = jax.random.truncated_normal(key, -4.0, 4.0, complete_shape, jnp.float32)
    scaled = random_part * MODEL_WIDTH ** (-0.5)
    key_columns = scaled[:, :, :HEAD_WIDTH] + drawn_columns(feature_sign, column_polarity, chosen)
    return jnp.concatenate([key_columns, scaled[:, :, HEAD_WIDTH:]], axis=2).astype(jnp.bfloat16)


def draw_q_weight(key, part):
    feature_sign, column_polarity, chosen = shared_pattern(key)
    key = jax.random.fold_in(key, 5)
    complete_shape = (MODEL_WIDTH, KEY_VALUE_HEADS, QUERIES_PER_KEY * HEAD_WIDTH)
    random_part = jax.random.truncated_normal(key, -4.0, 4.0, complete_shape, jnp.float32)
    planted = jnp.tile(drawn_columns(feature_sign, column_polarity, chosen), (1, 1, QUERIES_PER_KEY))
    return (random_part * MODEL_WIDTH ** (-0.5) + planted).astype(jnp.bfloat16)


def with_ends(array, own_key, least, high):
    spot = [jax.random.randint(jax.random.fold_in(own_key, axis), (), 0, length) for axis, length in enumerate(array.shape)]
    longest = array.shape.index(max(array.shape))
    beside = spot[:longest] + [(spot[longest] + 1) % array.shape[longest]] + spot[longest + 1:]
    return array.at[tuple(spot)].set(least).at[tuple(beside)].set(high)


def level_of(own_key, shape, shards, least, largest):
    factor_of, own = 1.0, jax.random.fold_in(own_key, 6)
    for axis_at, blocks in shards:
        heights = jnp.exp(jax.random.uniform(jax.random.fold_in(own, axis_at), (blocks,), jnp.float32, least / len(shards), largest / len(shards)))
        factor_of = factor_of * jnp.repeat(heights, shape[axis_at] // blocks).reshape([-1 if axis == axis_at else 1 for axis in range(len(shape))])
    return factor_of


def split_up(amount, total, most, skew):
    weights = [(1 << 20) // math.isqrt(rank ** skew) + 1 for rank in range(2, amount + 1)]
    surplus, counts = total - most - (amount - 1), [1] * (amount - 1)
    while surplus > 0:
        free = [i for i in range(amount - 1) if counts[i] < most]
        mass, budget = sum([weights[i] for i in free]), surplus
        for i in free:
            extra = min(most - counts[i], max(1, budget * weights[i] // mass), surplus)
            counts[i] = counts[i] + extra
            surplus = surplus - extra
    return np.array([most] + counts)


def ragged_sizes(own_key, count, total, most, lean):
    if count == 2:
        one = jax.random.randint(own_key, (), max(1, total - most), min(most, total - 1) + 1)
        return jnp.stack([one, total - one])
    sizes = jnp.asarray(split_up(count, total, most, lean), jnp.int32)
    twos = (count - 1) // 2
    donor, sink = sizes[1:1 + 2 * twos:2], sizes[2:2 + 2 * twos:2]
    slack = jnp.minimum(donor - 1, most - sink)
    shifted = jax.random.randint(jax.random.fold_in(own_key, 1), (twos,), 0, 1 << 20) % (slack + 1)
    sizes = sizes.at[1:1 + 2 * twos:2].set(donor - shifted).at[2:2 + 2 * twos:2].set(sink + shifted)
    return sizes[jax.random.permutation(jax.random.fold_in(own_key, 2), count)]


def shared_out(key, own, number, rows, count, top, bound, lean):
    ranking = jax.random.permutation(key, count)
    packed, usual = portions_of(count, rows * top, bound, lean, True), portions_of(count, rows * top, bound, lean, False)
    places = jnp.arange(count)

    def named(tallies, offset_by):
        used = int((tallies > 0).sum())
        fixed = max(1, used // 4)
        shifted = fixed + (places - fixed + offset_by * (used - fixed)) % max(1, count - fixed)
        return jnp.zeros((count,), jnp.int32).at[ranking[jnp.where(places < fixed, places, shifted)]].set(jnp.asarray(tallies, jnp.int32))

    tallies = jnp.where(number % 4 == 0, named(packed, number // 4), named(usual, number - number // 4 - 1))
    mixed = jax.random.permutation(jax.random.fold_in(own, 3), count)
    giver, receiver = mixed[0:count // 2 * 2:2], mixed[1:count // 2 * 2:2]
    room = jnp.minimum(tallies[giver] - 1, bound - tallies[receiver]) // 2
    room = jnp.where((giver == ranking[0]) | (receiver == ranking[0]) | (tallies[receiver] == 0), 0, jnp.maximum(room, 0))
    shifted = jax.random.randint(jax.random.fold_in(own, 4), (count // 2,), 0, 1 << 20) % (room + 1)
    tallies = tallies.at[giver].add(-shifted).at[receiver].add(shifted)
    members = jnp.searchsorted(jnp.cumsum(tallies), jnp.arange(rows * top), side="right").astype(jnp.int32)
    grid = members.reshape(top, rows).T
    grid = grid[jax.random.permutation(jax.random.fold_in(own, 1), rows)]
    offset_by = jax.random.randint(jax.random.fold_in(own, 2), (rows, 1), 0, top)
    return jnp.take_along_axis(grid, (jnp.arange(top)[None, :] + offset_by) % top, axis=1)


def portions_of(number_of, total, most, lean, full):
    portions = [(1 << 20) // math.isqrt(rank ** lean) + 1 for rank in range(1, number_of + 1)]
    largest = most if full else min(most, max(-(-total // number_of), total * portions[0] // sum(portions)))
    least = 1 if total - largest >= number_of - 1 else 0
    given, rest = [largest] + [least] * (number_of - 1), total - largest - least * (number_of - 1)
    while rest > 0:
        candidates = [i for i in range(1, number_of) if given[i] < largest] or [i for i in range(1, number_of) if given[i] < most]
        pool, remaining = sum([portions[i] for i in candidates]), rest
        for i in candidates:
            more = min(most - given[i], max(1, remaining * portions[i] // pool), rest)
            given[i] = given[i] + more
            rest = rest - more
    return np.array(given)


def centred(key, shape, scale, limit, shards=(), kind=jnp.bfloat16):
    drawn = scale * jax.random.normal(key, shape, jnp.float32)
    if shards:
        drawn = drawn * level_of(key, shape, shards, -0.22, 0.18)
    return jnp.clip(drawn, -limit, limit).astype(kind)


def setup_inputs(seed: int = 0) -> dict:
    keys = jax.random.split(jax.random.key(seed), 10)
    prompt_states = draw_prompt_states(jax.random.fold_in(keys[9], 71), 0)
    prompt_lengths = ragged_sizes(keys[1], PROMPTS, PROMPTS * LP // 2, LP, 2).astype(jnp.int32)
    decode_states = draw_decode_states(jax.random.fold_in(keys[9], 71), 0)
    sample_owner_keys = jax.random.split(jax.random.fold_in(keys[3], 1), SAMPLES // S_DEV)
    sample_owner_turns = jax.random.permutation(jax.random.fold_in(keys[3], 3), SAMPLES // S_DEV)
    sample_owner = jax.vmap(lambda own, number: shared_out(jax.random.fold_in(keys[3], 2), own, number, S_DEV, OWNERS, 1, CAP, 1))(sample_owner_keys, sample_owner_turns).reshape((SAMPLES, 1))
    sample_local = with_ends(jax.random.randint(keys[4], (SAMPLES,), 0, P_DEV), jax.random.fold_in(keys[4], 1), 0, P_DEV - 1).astype(jnp.int32)
    norm_gain = jnp.clip(jnp.exp(math.log(2.0) - 1.3862944 * jax.random.uniform(keys[5], (MODEL_WIDTH,), jnp.float32) ** level_of(keys[5], (MODEL_WIDTH,), ((0, 8),), -0.2, 0.2)), 0.5, 2.0)
    kv_weight = draw_kv_weight(jax.random.fold_in(keys[9], 71), 0)
    q_weight = draw_q_weight(jax.random.fold_in(keys[9], 71), 0)
    output_weight = centred(keys[8], (KEY_VALUE_HEADS, QUERIES_PER_KEY * HEAD_WIDTH, MODEL_WIDTH), (QUERIES_PER_KEY * HEAD_WIDTH) ** -0.5, 0.3125, ((0, 8),))
    return {"prompt_states": prompt_states, "prompt_lengths": prompt_lengths, "decode_states": decode_states, "sample_owner": sample_owner, "sample_local": sample_local, "norm_gain": norm_gain, "kv_weight": kv_weight, "q_weight": q_weight, "output_weight": output_weight}


EPSILON = 1e-06
HUGE_NEGATIVE = -1e+30

def rounded(values):
    narrow = values.astype(jnp.bfloat16)
    return lax.optimization_barrier(narrow).astype(jnp.float32)

def project(states, norm_gain, weight):
    widened = states.astype(jnp.float32)
    inverse = lax.rsqrt(lax.optimization_barrier(jnp.mean(widened * widened, axis=-1)) + EPSILON)
    scaled = rounded(widened * norm_gain)
    product = jnp.einsum('...d,dhc->...hc', scaled, weight.astype(jnp.float32))
    return (product * inverse[..., None, None]).astype(jnp.bfloat16)

def softmax_part(scores, usable, value_rows, pattern):
    scores = jnp.where(usable, scores, HUGE_NEGATIVE)
    highest = lax.optimization_barrier(jnp.max(scores, axis=-1))
    weights = jnp.where(usable, jnp.exp(scores - highest[..., None]), 0.0)
    weight_sum = lax.optimization_barrier(jnp.sum(weights, axis=-1))
    blended = jnp.einsum(pattern, rounded(weights), value_rows.astype(jnp.float32))
    return (highest, weight_sum, blended)

def prefix_part(queries, stored, lengths):
    head_size = queries.shape[-1]
    scores = jnp.einsum('nthqe,nlhe->nthql', queries.astype(jnp.float32), stored[..., :head_size].astype(jnp.float32)) * head_size ** (-0.5)
    positions = jnp.arange(stored.shape[1], dtype=jnp.int32)
    usable = (positions[None, :] < lengths[:, None])[:, None, None, None, :]
    return softmax_part(scores, usable, stored[..., head_size:], 'nthql,nlhe->nthqe')

def own_part(queries, own_rows):
    head_size = queries.shape[-1]
    scores = jnp.einsum('nthqe,nuhe->nthqu', queries.astype(jnp.float32), own_rows[..., :head_size].astype(jnp.float32)) * head_size ** (-0.5)
    step_ids = jnp.arange(queries.shape[1], dtype=jnp.int32)
    usable = (step_ids[None, :] <= step_ids[:, None])[None, :, None, None, :]
    return softmax_part(scores, usable, own_rows[..., head_size:], 'nthqu,nuhe->nthqe')

def merge_parts(former, latter):
    highest = jnp.maximum(former[0], latter[0])
    factor_one = jnp.exp(former[0] - highest)
    factor_two = jnp.exp(latter[0] - highest)
    numerator = former[2] * factor_one[..., None] + latter[2] * factor_two[..., None]
    denominator = former[1] * factor_one + latter[1] * factor_two
    return (numerator / denominator[..., None]).astype(jnp.bfloat16)

def reference(prompt_states, prompt_lengths, decode_states, sample_owner, sample_local, norm_gain, kv_weight, q_weight, output_weight):
    prompt_cache = project(prompt_states, norm_gain, kv_weight)
    queries = project(decode_states, norm_gain, q_weight)
    own_cache = project(decode_states, norm_gain, kv_weight)
    which = (sample_owner[:, 0] * P_DEV + sample_local).astype(jnp.int32)
    sample_count = decode_states.shape[0]
    step_count = decode_states.shape[1]
    out_weight = output_weight.astype(jnp.float32)

    def one_block(block):
        block_queries, block_own, block_which = block
        shaped = block_queries.reshape(block_queries.shape[:3] + (QUERIES_PER_KEY, HEAD_WIDTH))
        stored = jnp.take(prompt_cache, block_which, axis=0)
        lengths = jnp.take(prompt_lengths, block_which)
        attended = merge_parts(prefix_part(shaped, stored, lengths), own_part(shaped, block_own))
        flattened = attended.reshape(attended.shape[:3] + (QUERIES_PER_KEY * HEAD_WIDTH,))
        partial_value = rounded(jnp.einsum('nthc,hcd->nthd', flattened.astype(jnp.float32), out_weight))
        return lax.optimization_barrier(jnp.sum(partial_value, axis=2)).astype(jnp.bfloat16)
    blocks = (queries.reshape((N_DP, S_DEV) + queries.shape[1:]), own_cache.reshape((N_DP, S_DEV) + own_cache.shape[1:]), which.reshape(N_DP, S_DEV))
    result = lax.map(one_block, blocks)
    return result.reshape(sample_count, step_count, MODEL_WIDTH)
```

```python
import jax
import jax.numpy as jnp
from jax import lax
from jax.experimental import pallas as pl
from jax.experimental.pallas import tpu as pltpu
from jax.sharding import PartitionSpec as P

MESH = pl.DeviceIdType.MESH
F32 = jnp.float32
BF16 = jnp.bfloat16

MODEL_WIDTH = 5120
EPSILON = 1e-06
HUGE_NEGATIVE = -1e30

NX, NZ, NY, NC = 4, 8, 4, 2
NDP = NX * NZ
NT = NY * NC
D = 640
HEAD = 128
GROUP = 3
PROMPTS = 4
LP = 256
PR = PROMPTS * LP
HALF = PR // 2
DR = 256
DHALF = DR // 2
SLOTS = 16
WIDTH = GROUP * HEAD + 2 * HEAD
SLICE = 80

G_CORE = 0
G_UP_A, G_UP_B, G_DN_B, G_DN_A = 1, 2, 3, 4
G_UP_FA, G_DN_FB = 5, 6
G_REL = 7
SQ = 13
PS = 20
WY = 21
WZ_UP = 24
WZ_DN = 28
WX = 31
RP = 43
IDS, QX, RX = 49, 50, 51
AX = 52
WO = 53
RO = 57
N_SEM = 63


def nn(a, b):
    return lax.dot_general(a, b, (((1,), (0,)), ((), ())), preferred_element_type=F32)


def nt(a, b):
    return lax.dot_general(a, b, (((1,), (1,)), ((), ())), preferred_element_type=F32)


def iota(shape, dim):
    return lax.broadcasted_iota(jnp.int32, shape, dim)


def kernel(
    decode_hbm, prompt_hbm, gain_ref, which_ref, owner_row_ref, owner_col_ref, lengths_ref,
    kv_hbm, q_hbm, wo_hbm,
    out_ref,
    dec_raw, prm_raw, dg, ps, sg, ids, qw, kvw, wt, wob,
    rp_send, rp_recv, own_sum, kc, acc, qo, qr, ro_, rr, ax, rs_send, rs_recv,
    pid_ref, len_ref, rcol,
    ss, rs, ls,
):
    d = lax.axis_index("dp")
    t = lax.axis_index("tensor")
    z, x = d // NX, d % NX
    y, c = t // NC, t % NC
    oc = 1 - c

    def at_y(j):
        return (d, ((y + j) % NY) * NC + c)

    def at_z(j):
        return (((z + j) % NZ) * NX + x, t)

    def at_x(j):
        return (z * NX + (x + j) % NX, t)

    core = (d, y * NC + oc)
    up, dn = at_y(1), at_y(NY - 1)

    def block_of(j):
        return ((y + j) % NY) * NC + c

    def remote(src, dst, n, dev):
        return pltpu.make_async_remote_copy(
            src_ref=src, dst_ref=dst, send_sem=ss.at[n], recv_sem=rs.at[n],
            device_id=dev, device_id_type=MESH,
        )

    sent = []

    def send(src, dst, n, dev):
        copy = remote(src, dst, n, dev)
        copy.start()
        sent.append(copy)
        return copy

    l_dec = pltpu.make_async_copy(decode_hbm, dec_raw, ls.at[0])
    l_prm = pltpu.make_async_copy(prompt_hbm, prm_raw, ls.at[1])
    l_kv = pltpu.make_async_copy(kv_hbm, kvw, ls.at[2])
    l_q = pltpu.make_async_copy(q_hbm, qw, ls.at[3])
    l_wt = pltpu.make_async_copy(
        kv_hbm.at[pl.ds(pl.multiple_of(y * (2 * D), 2 * D), 2 * D)], wt.at[0], ls.at[4]
    )
    l_dec.start()
    l_prm.start()
    l_kv.start()
    l_wt.start()
    l_q.start()
    l_wo = []
    for b in range(NY):
        cols = pl.ds(pl.multiple_of((2 * b + c) * D, 128), D)
        copy = pltpu.make_async_copy(wo_hbm.at[:, cols], wob.at[0, b], ls.at[5 + b])
        copy.start()
        l_wo.append(copy)

    barrier = pltpu.get_barrier_semaphore()
    for k in range(1, NT):
        pl.semaphore_signal(barrier, inc=1, device_id=(d, (t + k) % NT), device_id_type=MESH)

    def greet(k, carry):
        pl.semaphore_signal(barrier, inc=1, device_id=((d + k) % NDP, t), device_id_type=MESH)
        return carry

    lax.fori_loop(1, NDP, greet, 0)
    pl.semaphore_wait(barrier, NT - 1 + NDP - 1)

    l_kv.wait()
    my_cols = pl.ds(pl.multiple_of((x // 2) * 128, 128), 128)
    my_row = ((x % 2) * NZ + z) * SLICE
    wy = {}
    for n, j in enumerate((2, 1, 3)):
        src_row = pl.multiple_of(((y + j) % NY) * (2 * D) + my_row, 16)
        wy[j] = send(
            kvw.at[pl.ds(src_row, SLICE), my_cols],
            wt.at[NY - j, pl.ds(pl.multiple_of(my_row, 16), SLICE), my_cols],
            WY + n, at_y(j),
        )

    l_dec.wait()
    dg[t] = (dec_raw[...].astype(F32) * gain_ref[...]).astype(BF16)
    A, B = pl.ds(0, DHALF), pl.ds(DHALF, DHALF)
    up_a = send(dg.at[t, A], dg.at[t, A], G_UP_A, up)
    dn_b = send(dg.at[t, B], dg.at[t, B], G_DN_B, dn)
    up_b = send(dg.at[t, B], dg.at[t, B], G_UP_B, up)
    dn_a = send(dg.at[t, A], dg.at[t, A], G_DN_A, dn)
    g_core = send(dg.at[t], dg.at[t], G_CORE, core)

    ids[d] = which_ref[...]

    def send_ids(k, carry):
        remote(ids.at[d], ids.at[d], IDS, ((d + k) % NDP, t)).start()
        return carry

    lax.fori_loop(1, NDP, send_ids, 0)

    ones = jnp.ones((8, D), BF16)

    def squares(value):
        sq = value * value
        high = sq.astype(BF16)
        low = (sq - high.astype(F32)).astype(BF16)
        return nt(ones, high) + nt(ones, low)

    row8 = iota((8, 128), 0)
    l_prm.wait()
    part = jnp.zeros((8, 128), F32)
    for i in range(PR // 128):
        value = prm_raw[i * 128 : (i + 1) * 128].astype(F32)
        ps[c, i * 128 : (i + 1) * 128] = (value * gain_ref[...]).astype(BF16)
        part = jnp.where(row8 == i, squares(value), part)
    ps_copy = send(ps.at[c], ps.at[c], PS, core)
    sg[t, 0:8] = part
    part = jnp.zeros((8, 128), F32)
    for i in range(DR // 128):
        value = dec_raw[i * 128 : (i + 1) * 128].astype(F32)
        part = jnp.where(row8 == i, squares(value), part)
    sg[t, 8:16] = part
    sq = [send(sg.at[t], sg.at[t], SQ + k - 1, (d, (t + k) % NT)) for k in range(1, NT)]

    def z_piece(j):
        row = pl.multiple_of(((x % 2) * NZ + (z + NZ + j) % NZ) * SLICE, 16)
        return wt.at[pl.ds(1, NY - 1), pl.ds(row, SLICE), my_cols]

    for j in (2, 1, 3):
        wy[j].wait_recv()
    for s in range(4):
        z_up = send(z_piece(-s), z_piece(-s), WZ_UP + s, at_z(1))
        if s < 3:
            z_dn = send(z_piece(s), z_piece(s), WZ_DN + s, at_z(NZ - 1))
        z_up.wait_recv()
        if s < 3:
            z_dn.wait_recv()

    def x_piece(slot, j, first, rows):
        xx = (x + NX + j) % NX
        row = pl.multiple_of((xx % 2) * D + first, 16)
        return wt.at[slot, pl.ds(row, rows), pl.ds(pl.multiple_of((xx // 2) * 128, 128), 128)]

    x_copies = {}
    for n, slot in enumerate((2, 1, 3)):
        whole = x_piece(slot, 0, 0, D)
        x_copies[slot] = [
            send(whole, whole, WX + 4 * n, at_x(1)),
            send(whole, whole, WX + 4 * n + 1, at_x(NX - 1)),
        ]

    def x_forward(n, slot):
        x_copies[slot][0].wait_recv()
        piece = x_piece(slot, -1, 0, D // 2)
        x_copies[slot].append(send(piece, piece, WX + 4 * n + 2, at_x(1)))
        x_copies[slot][1].wait_recv()
        piece = x_piece(slot, 1, D // 2, D // 2)
        x_copies[slot].append(send(piece, piece, WX + 4 * n + 3, at_x(NX - 1)))

    def x_finish(slot):
        x_copies[slot][2].wait_recv()
        x_copies[slot][3].wait_recv()

    below, above, opposite = block_of(NY - 1), block_of(1), block_of(2)
    up_a.wait_recv()
    up_fa = send(dg.at[below, A], dg.at[below, A], G_UP_FA, up)
    dn_b.wait_recv()
    dn_fb = send(dg.at[above, B], dg.at[above, B], G_DN_FB, dn)
    relays = [
        send(dg.at[below, A], dg.at[below, A], G_REL, core),
        send(dg.at[above, B], dg.at[above, B], G_REL + 1, core),
    ]
    up_b.wait_recv()
    relays.append(send(dg.at[below, B], dg.at[below, B], G_REL + 2, core))
    dn_a.wait_recv()
    relays.append(send(dg.at[above, A], dg.at[above, A], G_REL + 3, core))

    r256, c256 = iota((DR, DR), 0), iota((DR, DR), 1)
    same = (owner_col_ref[...] == owner_row_ref[...]) & ((r256 & 3) == (c256 & 3))
    rank_row = jnp.sum(jnp.where(same & (r256 < c256), 1, 0), axis=0, keepdims=True)
    rank_col = jnp.sum(jnp.where(same & (c256 < r256), 1, 0), axis=1, keepdims=True)
    lane_row = iota((1, DR), 1)
    lane_col = iota((DR, 1), 0)
    target_row = owner_row_ref[...] * SLOTS + rank_row * 4 + (lane_row & 3)
    target_col = owner_col_ref[...] * SLOTS + rank_col * 4 + (lane_col & 3)
    n_slots = NDP * SLOTS

    up_fa.wait_recv()
    relays.append(send(dg.at[opposite, A], dg.at[opposite, A], G_REL + 4, core))
    dn_fb.wait_recv()
    relays.append(send(dg.at[opposite, B], dg.at[opposite, B], G_REL + 5, core))

    x_forward(0, 2)
    x_forward(1, 1)
    x_forward(2, 3)

    wo_copies = []
    for b in range(NY):
        cols = pl.ds(pl.multiple_of((2 * b + oc) * D, 128), D)
        wo_copies.append(send(wo_hbm.at[:, cols], wob.at[1, b], WO + b, core))

    for copy in sq:
        copy.wait_recv()
    total = sg[0]
    for k in range(1, NT):
        total = total + sg[k]
    factor = lax.rsqrt(total / MODEL_WIDTH + EPSILON)
    for i in range((PR + DR) // 128):
        rcol[i * 128 : (i + 1) * 128] = jnp.broadcast_to(factor[i : i + 1], (128, 128)).T

    g_core.wait_recv()
    for copy in relays:
        copy.wait_recv()
    l_q.wait()

    def project(k, carry):
        rows = pl.ds(pl.multiple_of(k * D, D), D)
        block = dg[k]
        add_q = nn(block, qw[rows])
        add_kv = nn(block, kvw[rows])

        @pl.when(k == 0)
        def _():
            acc[:, : GROUP * HEAD] = add_q
            acc[:, GROUP * HEAD :] = add_kv

        @pl.when(k > 0)
        def _():
            acc[:, : GROUP * HEAD] += add_q
            acc[:, GROUP * HEAD :] += add_kv

        return carry

    lax.fori_loop(0, NT, project, 0)
    scale = rcol[PR : PR + DR]
    projected = jnp.concatenate(
        [(acc[:, i * 128 : (i + 1) * 128] * scale).astype(BF16) for i in range(WIDTH // 128)], axis=1
    )
    for i in range(4):
        rows = iota((n_slots // 4, DR), 0) + i * (n_slots // 4)
        pick = jnp.where(rows == target_row, 1.0, 0.0).astype(BF16)
        placed = nn(pick, projected).astype(BF16)
        qo[i * 8 : (i + 1) * 8] = placed.reshape(8, SLOTS, WIDTH)
    qr[d] = qo[d]

    def send_q(k, carry):
        to = (d + k) % NDP
        remote(qo.at[to], qr.at[d], QX, (to, t)).start()
        return carry

    lax.fori_loop(1, NDP, send_q, 0)

    ps_copy.wait_recv()
    l_wt.wait()

    def partial(j, row, rows):
        at = pl.ds(pl.multiple_of(row, rows), rows)
        return nn(ps[0, at], wt[j, :D]) + nn(ps[1, at], wt[j, D:])

    def fill(n, j, base, extra):
        def one(i, carry):
            at = pl.ds(pl.multiple_of(i * 128, 128), 128)
            value = partial(j, base + i * 128, 128)
            if extra is not None:
                value = value + rp_recv[extra, at].astype(F32)
            rp_send[n, at] = value.astype(BF16)
            return carry

        lax.fori_loop(0, HALF // 128, one, 0)

    def rp(n, dev):
        return send(rp_send.at[n], rp_recv.at[n], RP + n, dev)

    x_finish(2)
    fill(0, 2, 0, None)
    rp0 = rp(0, dn)
    fill(1, 2, HALF, None)
    rp1 = rp(1, up)
    x_finish(1)
    fill(2, 1, 0, None)
    rp2 = rp(2, up)
    x_finish(3)
    fill(3, 3, HALF, None)
    rp3 = rp(3, dn)
    rp0.wait_recv()
    fill(4, 3, 0, 0)
    rp4 = rp(4, dn)
    rp1.wait_recv()
    fill(5, 1, HALF, 1)
    rp5 = rp(5, up)

    def own_rows(i, carry):
        at = pl.ds(pl.multiple_of(i * 128, 128), 128)
        own_sum[at] = partial(0, i * 128, 128)
        return carry

    lax.fori_loop(0, PR // 128, own_rows, 0)

    pltpu.make_async_copy(ids.at[pl.ds(0, NDP - 1)], ids.at[pl.ds(0, NDP - 1)], rs.at[IDS]).wait()
    which = jnp.concatenate([ids[s] for s in range(NDP)], axis=0)
    local = which - (PROMPTS * d).astype(F32)
    match = (local >= 0.0) & (local < float(PROMPTS))
    before = jnp.where(iota((128, 128), 0) < iota((128, 128), 1), 1.0, 0.0).astype(BF16)
    rank = nn(jnp.where(match, 1.0, 0.0).astype(BF16), before)
    lane = iota((NDP, 128), 1)
    table = jnp.zeros((NDP, 128), F32)
    for k in range(4):
        at_k = jnp.sum(
            jnp.where(match & (rank == float(k)), local, 0.0), axis=1, keepdims=True
        )
        table = jnp.where(lane == k, at_k, table)
    table = table.astype(BF16)
    for i in range(4):
        sub = iota((128, NDP), 0)
        spread = jnp.where((sub >> 4) + 8 * i == iota((128, NDP), 1), 1.0, 0.0).astype(BF16)
        wide = nn(spread, table)
        mine = iota((128, 128), 1) == ((iota((128, 128), 0) >> 2) & 3)
        pid = jnp.sum(jnp.where(mine, wide, 0.0), axis=1, keepdims=True)
        pid_ref[i * 128 : (i + 1) * 128] = jnp.broadcast_to(pid, (128, 128))
        lens = jnp.zeros((128, 1), F32)
        for p in range(PROMPTS):
            lens = jnp.where(pid == float(p), lengths_ref[PROMPTS * d + p].astype(F32), lens)
        len_ref[i * 128 : (i + 1) * 128] = jnp.broadcast_to(lens, (128, 128))

    rp2.wait_recv()
    rp4.wait_recv()

    def finish_rows(base, one_slot, two_slot):
        def one(i, carry):
            at = pl.ds(pl.multiple_of(i * 128, 128), 128)
            there = pl.ds(pl.multiple_of(base + i * 128, 128), 128)
            value = own_sum[there] + rp_recv[one_slot, at].astype(F32) + rp_recv[two_slot, at].astype(F32)
            factor = rcol[there]
            kc[there, :HEAD] = (value[:, :HEAD] * factor).astype(BF16)
            kc[there, HEAD:] = (value[:, HEAD:] * factor).astype(BF16)
            return carry

        lax.fori_loop(0, HALF // 128, one, 0)

    finish_rows(0, 2, 4)
    rp3.wait_recv()
    rp5.wait_recv()
    finish_rows(HALF, 3, 5)

    pltpu.make_async_copy(qr.at[pl.ds(0, NDP - 1)], qr.at[pl.ds(0, NDP - 1)], rs.at[QX]).wait()
    root = float(HEAD) ** -0.5

    def attend(i, carry):
        at = pl.ds(pl.multiple_of(i * 128, 128), 128)
        sources = pl.ds(pl.multiple_of(i * 8, 8), 8)
        rows = qr[sources].reshape(128, WIDTH)
        own_k = rows[:, GROUP * HEAD : GROUP * HEAD + HEAD]
        own_v = rows[:, GROUP * HEAD + HEAD :]
        pid = pid_ref[at, 0:1]
        lens = len_ref[at, 0:1]
        live = iota((128, LP), 1).astype(F32) < lens
        r, cc = iota((128, 128), 0), iota((128, 128), 1)
        usable = ((r >> 2) == (cc >> 2)) & ((cc & 3) <= (r & 3))
        results = []
        for h in range(GROUP):
            query = rows[:, h * HEAD : (h + 1) * HEAD]
            scores = nt(query, kc[0:LP, :HEAD])
            for p in range(1, PROMPTS):
                scores = jnp.where(pid == float(p), nt(query, kc[p * LP : (p + 1) * LP, :HEAD]), scores)
            scores = jnp.where(live, scores * root, HUGE_NEGATIVE)
            top = jnp.max(scores, axis=1, keepdims=True)
            weights = jnp.where(live, jnp.exp(scores - top), 0.0)
            mass = jnp.sum(weights, axis=1, keepdims=True)
            blended = jnp.zeros((128, HEAD), F32)
            for p in range(PROMPTS):
                masked = jnp.where(pid == float(p), weights, 0.0).astype(BF16)
                blended = blended + nn(masked, kc[p * LP : (p + 1) * LP, HEAD:])
            own = jnp.where(usable, nt(query, own_k) * root, HUGE_NEGATIVE)
            own_top = jnp.max(own, axis=1, keepdims=True)
            own_weights = jnp.where(usable, jnp.exp(own - own_top), 0.0)
            own_mass = jnp.sum(own_weights, axis=1, keepdims=True)
            own_blended = nn(own_weights.astype(BF16), own_v)
            highest = jnp.maximum(top, own_top)
            one, two = jnp.exp(top - highest), jnp.exp(own_top - highest)
            numerator = blended * one + own_blended * two
            denominator = mass * one + own_mass * two
            results.append((numerator / denominator).astype(BF16))
        ro_[sources] = jnp.concatenate(results, axis=1).reshape(8, SLOTS, GROUP * HEAD)
        return carry

    lax.fori_loop(0, 4, attend, 0)
    rr[d] = ro_[d]

    def send_back(k, carry):
        to = (d + k) % NDP
        remote(ro_.at[to], rr.at[d], RX, (to, t)).start()
        return carry

    lax.fori_loop(1, NDP, send_back, 0)
    pltpu.make_async_copy(rr.at[pl.ds(0, NDP - 1)], rr.at[pl.ds(0, NDP - 1)], rs.at[RX]).wait()

    take = jnp.where(iota((DR, n_slots), 1) == target_col, 1.0, 0.0).astype(BF16)
    ax[c] = nn(take, rr[...].reshape(n_slots, GROUP * HEAD)).astype(BF16)
    ax_copy = send(ax.at[c], ax.at[c], AX, core)
    for copy in l_wo:
        copy.wait()
    for copy in wo_copies:
        copy.wait_recv()
    ax_copy.wait_recv()

    def out_partial(j, row):
        b = (y + j) % NY
        at = pl.ds(row, DHALF)
        return nn(ax[c, at], wob[0, b]) + nn(ax[oc, at], wob[1, b])

    def out_send(n, j, row, extra, dev):
        value = out_partial(j, row)
        if extra is not None:
            value = value + rs_recv[extra].astype(F32)
        rs_send[n] = value.astype(BF16)
        return send(rs_send.at[n], rs_recv.at[n], RO + n, dev)

    o0 = out_send(0, 2, 0, None, dn)
    o1 = out_send(1, 2, DHALF, None, up)
    o2 = out_send(2, 1, 0, None, up)
    o3 = out_send(3, 3, DHALF, None, dn)
    o0.wait_recv()
    o4 = out_send(4, 3, 0, 0, dn)
    o1.wait_recv()
    o5 = out_send(5, 1, DHALF, 1, up)
    own_a = out_partial(0, 0)
    o2.wait_recv()
    o4.wait_recv()
    out_ref[:DHALF] = (own_a + rs_recv[2].astype(F32) + rs_recv[4].astype(F32)).astype(BF16)
    own_b = out_partial(0, DHALF)
    o3.wait_recv()
    o5.wait_recv()
    out_ref[DHALF:] = (own_b + rs_recv[3].astype(F32) + rs_recv[5].astype(F32)).astype(BF16)

    for copy in sent:
        copy.wait_send()
    for ref, n in ((ids, IDS), (qo, QX), (ro_, RX)):
        pltpu.make_async_copy(ref.at[pl.ds(0, NDP - 1)], ref.at[pl.ds(0, NDP - 1)], ss.at[n]).wait()


def shards(
    prompt_states, prompt_lengths, decode_states, sample_owner, sample_local,
    norm_gain, kv_weight, q_weight, output_weight,
):
    owner = sample_owner[:, 0]
    which = (owner * PROMPTS + sample_local).astype(F32)
    which = jnp.concatenate([which, jnp.full((64,), -1.0, F32)]).reshape(1, 128)
    owners = jnp.repeat(owner, 4)
    vmem = pl.BlockSpec(memory_space=pltpu.VMEM)
    hbm = pl.BlockSpec(memory_space=pl.ANY)
    out = pl.pallas_call(
        kernel,
        out_shape=jax.ShapeDtypeStruct((DR, D), BF16),
        in_specs=[hbm, hbm, vmem, vmem, vmem, vmem, pl.BlockSpec(memory_space=pltpu.SMEM), hbm, hbm, hbm],
        out_specs=vmem,
        scratch_shapes=[
            pltpu.VMEM((DR, D), BF16),
            pltpu.VMEM((PR, D), BF16),
            pltpu.VMEM((NT, DR, D), BF16),
            pltpu.VMEM((NC, PR, D), BF16),
            pltpu.VMEM((NT, 16, 128), F32),
            pltpu.VMEM((NDP, 1, 128), F32),
            pltpu.VMEM((MODEL_WIDTH, GROUP * HEAD), BF16),
            pltpu.VMEM((MODEL_WIDTH, 2 * HEAD), BF16),
            pltpu.VMEM((NY, 2 * D, 2 * HEAD), BF16),
            pltpu.VMEM((NC, NY, GROUP * HEAD, D), BF16),
            pltpu.VMEM((6, HALF, 2 * HEAD), BF16),
            pltpu.VMEM((6, HALF, 2 * HEAD), BF16),
            pltpu.VMEM((PR, 2 * HEAD), F32),
            pltpu.VMEM((PR, 2 * HEAD), BF16),
            pltpu.VMEM((DR, WIDTH), F32),
            pltpu.VMEM((NDP, SLOTS, WIDTH), BF16),
            pltpu.VMEM((NDP, SLOTS, WIDTH), BF16),
            pltpu.VMEM((NDP, SLOTS, GROUP * HEAD), BF16),
            pltpu.VMEM((NDP, SLOTS, GROUP * HEAD), BF16),
            pltpu.VMEM((NC, DR, GROUP * HEAD), BF16),
            pltpu.VMEM((6, DHALF, D), BF16),
            pltpu.VMEM((6, DHALF, D), BF16),
            pltpu.VMEM((NDP * SLOTS, 128), F32),
            pltpu.VMEM((NDP * SLOTS, 128), F32),
            pltpu.VMEM((PR + DR, 128), F32),
            pltpu.SemaphoreType.DMA((N_SEM,)),
            pltpu.SemaphoreType.DMA((N_SEM,)),
            pltpu.SemaphoreType.DMA((9,)),
        ],
        compiler_params=pltpu.CompilerParams(
            collective_id=0, has_side_effects=True, vmem_limit_bytes=56 * 1024 * 1024
        ),
    )(
        decode_states.reshape(DR, D),
        prompt_states.reshape(PR, D),
        norm_gain.reshape(1, D),
        which.reshape(1, 128),
        owners.reshape(1, DR),
        owners.reshape(DR, 1),
        prompt_lengths,
        kv_weight.reshape(MODEL_WIDTH, 2 * HEAD),
        q_weight.reshape(MODEL_WIDTH, GROUP * HEAD),
        output_weight.reshape(GROUP * HEAD, MODEL_WIDTH),
    )
    return out.reshape(64, 4, D)


def solution(mesh):
    placed = (
        P("dp", None, "tensor"),
        P(),
        P("dp", None, "tensor"),
        P("dp", None),
        P("dp"),
        P("tensor"),
        P(None, "tensor", None),
        P(None, "tensor", None),
        P("tensor", None, None),
    )
    return jax.shard_map(
        shards, mesh=mesh, in_specs=placed, out_specs=P("dp", None, "tensor"), check_vma=False
    )
```

```python
import jax
import jax.numpy as jnp
from jax import lax
from jax.experimental import pallas as pl
from jax.experimental.pallas import tpu as pltpu
from jax.sharding import PartitionSpec as P

MESH = pl.DeviceIdType.MESH
F32 = jnp.float32
BF16 = jnp.bfloat16

MODEL_WIDTH = 5120
EPSILON = 1e-06
HUGE_NEGATIVE = -1e30

NX, NZ, NY, NC = 4, 8, 4, 2
NDP = NX * NZ
NT = NY * NC
D = 640
HEAD = 128
GROUP = 3
PROMPTS = 4
LP = 256
PR = PROMPTS * LP
HALF = PR // 2
DR = 256
DHALF = DR // 2
SLOTS = 16
WIDTH = GROUP * HEAD + 2 * HEAD
SLICE = 80

A_ROWS = 48

IDS, QX, RX = 0, 1, 2
N_SEM = 160


def nn(a, b):
    return lax.dot_general(a, b, (((1,), (0,)), ((), ())), preferred_element_type=F32)


def nt(a, b):
    return lax.dot_general(a, b, (((1,), (1,)), ((), ())), preferred_element_type=F32)


def iota(shape, dim):
    return lax.broadcasted_iota(jnp.int32, shape, dim)


def kernel(
    decode_hbm, prompt_hbm, gain_ref, owner_ref, local_ref, lengths_ref,
    kv_hbm, q_hbm, wo_hbm,
    out_ref,
    dec_raw, prm_raw, dg, ps, sg, ids, qw, kvw, wt, wob,
    rp_send, rp_recv, own_sum, kt, vc, acc, qo, qr, ro_, rr, ax, rs_send, rs_recv,
    pid_ref, len_ref, rcol,
    ss, rs, ls,
):
    d = lax.axis_index("dp")
    t = lax.axis_index("tensor")
    z, x = d // NX, d % NX
    y, c = t // NC, t % NC
    oc = 1 - c

    def at_y(j):
        return (d, ((y + j) % NY) * NC + c)

    def at_z(j):
        return (((z + j) % NZ) * NX + x, t)

    def at_x(j):
        return (z * NX + (x + j) % NX, t)

    core = (d, y * NC + oc)
    up, dn = at_y(1), at_y(NY - 1)

    def block_of(j):
        return ((y + j) % NY) * NC + c

    def remote(src, dst, n, dev):
        return pltpu.make_async_remote_copy(
            src_ref=src, dst_ref=dst, send_sem=ss.at[n], recv_sem=rs.at[n],
            device_id=dev, device_id_type=MESH,
        )

    sent = []

    def send(src, dst, dev):
        copy = remote(src, dst, 3 + len(sent), dev)
        copy.start()
        sent.append(copy)
        return copy

    def local_copy(src, dst, n):
        copy = pltpu.make_async_copy(src, dst, ls.at[n])
        copy.start()
        return copy

    def many(ref, sem):
        part = ref.at[pl.ds(0, NDP - 1)]
        return pltpu.make_async_copy(part, part, sem)

    def send_many(ref, to_ref, n, per_target):
        def one(k, carry):
            to = (d + k) % NDP
            remote(ref.at[to if per_target else d], to_ref.at[d], n, (to, t)).start()
            return carry

        lax.fori_loop(1, NDP, one, 0)

    def wait_many(to_ref, n):
        many(to_ref, rs.at[n]).wait()

    l_dec = local_copy(decode_hbm, dec_raw, 0)
    l_kv = local_copy(kv_hbm, kvw, 2)
    l_prm = local_copy(prompt_hbm, prm_raw, 1)
    l_q = local_copy(q_hbm, qw, 3)
    l_wt = local_copy(kv_hbm.at[y], wt.at[0], 4)
    l_wo = []
    for b in range(NY):
        cols = pl.ds(pl.multiple_of((2 * b + c) * D, 128), D)
        l_wo.append(local_copy(wo_hbm.at[:, cols], wob.at[0, b], 5 + b))

    barrier = pltpu.get_barrier_semaphore()
    for k in range(1, NT):
        pl.semaphore_signal(barrier, inc=1, device_id=(d, (t + k) % NT), device_id_type=MESH)

    def greet(k, carry):
        pl.semaphore_signal(barrier, inc=1, device_id=((d + k) % NDP, t), device_id_type=MESH)
        return carry

    lax.fori_loop(1, NDP, greet, 0)
    pl.semaphore_wait(barrier, NT - 1 + NDP - 1)

    xb, my_cols = x % 2, pl.ds(pl.multiple_of((x // 2) * 128, 128), 128)
    slots = (2, 1, 3)
    wy = {}
    for j in slots:
        wy[j] = send(
            kv_hbm.at[(y + j) % NY, xb, z, :, my_cols], wt.at[NY - j, xb, z, :, my_cols], at_y(j)
        )
    arrives = {j: wy[NY - j] for j in slots}

    l_dec.wait()
    gain = gain_ref[...].reshape(1, D)
    decode = dec_raw[...].astype(F32).reshape(DR, D)
    dg[t] = (decode * gain).astype(BF16)
    A, B = pl.ds(0, DHALF), pl.ds(DHALF, DHALF)

    def block(k, rows, dev):
        return send(dg.at[k, rows], dg.at[k, rows], dev)

    up_a = block(t, A, up)
    dn_b = block(t, B, dn)
    up_b = block(t, B, up)
    dn_a = block(t, A, dn)
    g_core = send(dg.at[t], dg.at[t], core)

    def same(ref, dev):
        return send(ref, ref, dev)

    up_z, dn_z, up_x, dn_x = at_z(1), at_z(NZ - 1), at_x(1), at_x(NX - 1)

    def a_piece(slot, j, first=0, rows=A_ROWS):
        return wt.at[slot, xb, (z + NZ + j) % NZ, pl.ds(first, rows), my_cols]

    def b_piece(slot, j, first=A_ROWS, rows=SLICE - A_ROWS):
        return wt.at[slot, :, (z + NZ + j) % NZ, pl.ds(first, rows)]

    def x_piece(slot, j, zs, rows):
        xx = (x + NX + j) % NX
        cols = pl.ds(pl.multiple_of((xx // 2) * 128, 128), 128)
        return wt.at[slot, xx % 2, zs, rows, cols]

    here = pl.ds(z, 1)
    a_rows, b_rows = pl.ds(0, A_ROWS), pl.ds(A_ROWS, SLICE - A_ROWS)
    b_mid = A_ROWS + (SLICE - A_ROWS) // 2
    az, ax_, bz, bx = {}, {}, {}, {}
    for slot in slots:
        arrives[slot].wait_recv()
        az[slot] = same(a_piece(slot, 0), up_z), same(a_piece(slot, 0), dn_z)
        piece = x_piece(slot, 0, here, b_rows)
        bx[slot] = same(piece, up_x), same(piece, dn_x)

    def a_step(slot, step):
        az[slot][0].wait_recv()
        az[slot][1].wait_recv()
        if step < 3:
            az[slot] = same(a_piece(slot, -step), up_z), same(a_piece(slot, step), dn_z)
        elif step == 3:
            az[slot] = (
                same(a_piece(slot, -3, 0, 32), up_z), same(a_piece(slot, 3, 32, A_ROWS - 32), dn_z)
            )

    def b_step(slot, step):
        bz[slot][0].wait_recv()
        bz[slot][1].wait_recv()
        if step < 3:
            bz[slot] = same(b_piece(slot, -step), up_z), same(b_piece(slot, step), dn_z)
        elif step == 3:
            bz[slot] = (
                same(b_piece(slot, -3, A_ROWS, b_mid - A_ROWS), up_z),
                same(b_piece(slot, 3, b_mid, SLICE - b_mid), dn_z),
            )

    mine = (owner_ref[...] * PROMPTS + local_ref[...]).astype(F32)
    ids[d] = jnp.concatenate([mine, jnp.full((1, 64), -1.0, F32)], axis=1)
    send_many(ids, ids, IDS, False)

    ones = jnp.ones((8, D), BF16)

    def squares(value):
        sq = value * value
        high = sq.astype(BF16)
        low = (sq - high.astype(F32)).astype(BF16)
        return nt(ones, high) + nt(ones, low)

    row8 = iota((8, 128), 0)
    parts = [jnp.zeros((8, 128), F32)]

    def prompt_block(i):
        value = prm_raw[i * 128 : (i + 1) * 128].astype(F32)
        ps[c, i * 128 : (i + 1) * 128] = (value * gain).astype(BF16)
        parts[0] = jnp.where(row8 == i, squares(value), parts[0])

    l_prm.wait()
    prompt_block(0)
    prompt_block(1)
    for slot in slots:
        a_step(slot, 1)
        bx[slot][0].wait_recv()
        bx[slot][1].wait_recv()
        bx[slot] = (
            same(x_piece(slot, -1, here, pl.ds(A_ROWS, b_mid - A_ROWS)), up_x),
            same(x_piece(slot, 1, here, pl.ds(b_mid, SLICE - b_mid)), dn_x),
        )
    prompt_block(2)
    prompt_block(3)
    for slot in slots:
        a_step(slot, 2)
        bx[slot][0].wait_recv()
        bx[slot][1].wait_recv()
        bz[slot] = same(b_piece(slot, 0), up_z), same(b_piece(slot, 0), dn_z)
    prompt_block(4)
    prompt_block(5)

    below, above, opposite = block_of(NY - 1), block_of(1), block_of(2)
    up_a.wait_recv()
    up_fa = block(below, A, up)
    dn_b.wait_recv()
    dn_fb = block(above, B, dn)
    relays = [block(below, A, core), block(above, B, core)]
    prompt_block(6)
    prompt_block(7)
    ps_copy = same(ps.at[c], core)
    sg[t, 0:8] = parts[0]
    part = jnp.zeros((8, 128), F32)
    for i in range(DR // 128):
        part = jnp.where(row8 == i, squares(decode[i * 128 : (i + 1) * 128]), part)
    sg[t, 8:16] = part
    sq = [same(sg.at[t], (d, (t + k) % NT)) for k in range(1, NT)]

    for slot in slots:
        a_step(slot, 3)
        b_step(slot, 1)
    up_b.wait_recv()
    relays.append(block(below, B, core))
    dn_a.wait_recv()
    relays.append(block(above, A, core))

    l_q.wait()
    l_kv.wait()

    def project(k, first=False):
        add_q = nn(dg[k], qw[k])
        add_kv = nn(dg[k], kvw[k // 2, k % 2].reshape(D, 2 * HEAD))
        if first:
            acc[:, : GROUP * HEAD] = add_q
            acc[:, GROUP * HEAD :] = add_kv
        else:
            acc[:, : GROUP * HEAD] += add_q
            acc[:, GROUP * HEAD :] += add_kv

    project(t, True)
    for slot in slots:
        a_step(slot, 4)
        whole = x_piece(slot, 0, pl.ds(0, NZ), a_rows)
        ax_[slot] = same(whole, up_x), same(whole, dn_x)
        b_step(slot, 2)
    project(below)
    project(above)
    up_fa.wait_recv()
    relays.append(block(opposite, A, core))
    dn_fb.wait_recv()
    relays.append(block(opposite, B, core))
    for slot in slots:
        ax_[slot][0].wait_recv()
        ax_[slot][1].wait_recv()
        ax_[slot] = (
            same(x_piece(slot, -1, pl.ds(0, NZ // 2), a_rows), up_x),
            same(x_piece(slot, 1, pl.ds(NZ // 2, NZ // 2), a_rows), dn_x),
        )
        b_step(slot, 3)

    def slot_ready(slot):
        ax_[slot][0].wait_recv()
        ax_[slot][1].wait_recv()
        b_step(slot, 4)

    project(opposite)
    g_core.wait_recv()
    for copy in relays:
        copy.wait_recv()
    for j in range(NY):
        project(((y + j) % NY) * NC + oc)

    r256, c256 = iota((DR, DR), 0), iota((DR, DR), 1)
    owners = jnp.broadcast_to(owner_ref[...].astype(F32), (8, 64)).astype(BF16)
    spread = jnp.where(iota((64, DR), 0) == (iota((64, DR), 1) >> 2), 1.0, 0.0).astype(BF16)
    owner_row = nn(owners, spread)[0:1].astype(jnp.int32)
    spread = jnp.where((iota((DR, 64), 0) >> 2) == iota((DR, 64), 1), 1.0, 0.0).astype(BF16)
    owner_col = nt(spread, owners)[:, 0:1].astype(jnp.int32)
    alike = (owner_col == owner_row) & ((r256 & 3) == (c256 & 3))
    rank_row = jnp.sum(jnp.where(alike & (r256 < c256), 1, 0), axis=0, keepdims=True)
    rank_col = jnp.sum(jnp.where(alike & (c256 < r256), 1, 0), axis=1, keepdims=True)
    lane_row = iota((1, DR), 1)
    lane_col = iota((DR, 1), 0)
    target_row = owner_row * SLOTS + rank_row * 4 + (lane_row & 3)
    target_col = owner_col * SLOTS + rank_col * 4 + (lane_col & 3)
    n_slots = NDP * SLOTS

    for copy in sq:
        copy.wait_recv()
    total = sg[0]
    for k in range(1, NT):
        total = total + sg[k]
    factor = lax.rsqrt(total / MODEL_WIDTH + EPSILON)
    for i in range((PR + DR) // 128):
        rcol[i * 128 : (i + 1) * 128] = jnp.broadcast_to(factor[i : i + 1], (128, 128)).T

    scale = rcol[PR : PR + DR]
    projected = jnp.concatenate(
        [(acc[:, i * 128 : (i + 1) * 128] * scale).astype(BF16) for i in range(WIDTH // 128)], axis=1
    )
    for i in range(4):
        rows = iota((n_slots // 4, DR), 0) + i * (n_slots // 4)
        pick = jnp.where(rows == target_row, 1.0, 0.0).astype(BF16)
        placed = nn(pick, projected).astype(BF16)
        qo[i * 8 : (i + 1) * 8] = placed.reshape(8, SLOTS, WIDTH)
    qr[d] = qo[d]
    send_many(qo, qr, QX, True)

    ps_copy.wait_recv()
    l_wt.wait()

    def partial(j, row, rows):
        at = pl.ds(pl.multiple_of(row, rows), rows)
        return nn(ps[0, at], wt[j, 0].reshape(D, 2 * HEAD)) + nn(ps[1, at], wt[j, 1].reshape(D, 2 * HEAD))

    def fill(n, j, base, extra):
        def one(i, carry):
            at = pl.ds(pl.multiple_of(i * 128, 128), 128)
            value = partial(j, base + i * 128, 128)
            if extra is not None:
                value = value + rp_recv[extra, at].astype(F32)
            rp_send[n, at] = value.astype(BF16)
            return carry

        lax.fori_loop(0, HALF // 128, one, 0)

    def rp(n, dev):
        return send(rp_send.at[n], rp_recv.at[n], dev)

    slot_ready(2)
    fill(0, 2, 0, None)
    rp0 = rp(0, dn)
    fill(1, 2, HALF, None)
    rp1 = rp(1, up)
    slot_ready(1)
    fill(2, 1, 0, None)
    rp2 = rp(2, up)
    slot_ready(3)
    fill(3, 3, HALF, None)
    rp3 = rp(3, dn)
    rp0.wait_recv()
    fill(4, 3, 0, 0)
    rp4 = rp(4, dn)
    rp1.wait_recv()
    fill(5, 1, HALF, 1)
    rp5 = rp(5, up)

    def own_rows(i, carry):
        at = pl.ds(pl.multiple_of(i * 128, 128), 128)
        own_sum[at] = partial(0, i * 128, 128)
        return carry

    lax.fori_loop(0, PR // 128, own_rows, 0)

    wo_copies = []
    for b in range(NY):
        cols = pl.ds(pl.multiple_of((2 * b + oc) * D, 128), D)
        wo_copies.append(send(wo_hbm.at[:, cols], wob.at[1, b], core))

    wait_many(ids, IDS)
    which = jnp.concatenate([ids[s] for s in range(NDP)], axis=0)
    local = which - (PROMPTS * d).astype(F32)
    match = (local >= 0.0) & (local < float(PROMPTS))
    before = jnp.where(iota((128, 128), 0) < iota((128, 128), 1), 1.0, 0.0).astype(BF16)
    rank = nn(jnp.where(match, 1.0, 0.0).astype(BF16), before)
    lane = iota((NDP, 128), 1)
    table = jnp.zeros((NDP, 128), F32)
    for k in range(4):
        at_k = jnp.sum(
            jnp.where(match & (rank == float(k)), local, 0.0), axis=1, keepdims=True
        )
        table = jnp.where(lane == k, at_k, table)
    table = table.astype(BF16)
    for i in range(4):
        sub = iota((128, NDP), 0)
        spread = jnp.where((sub >> 4) + 8 * i == iota((128, NDP), 1), 1.0, 0.0).astype(BF16)
        wide = nn(spread, table)
        mine = iota((128, 128), 1) == ((iota((128, 128), 0) >> 2) & 3)
        pid = jnp.sum(jnp.where(mine, wide, 0.0), axis=1, keepdims=True)
        pid_ref[i * 128 : (i + 1) * 128] = jnp.broadcast_to(pid, (128, 128))
        lens = jnp.zeros((128, 1), F32)
        for p in range(PROMPTS):
            lens = jnp.where(pid == float(p), lengths_ref[PROMPTS * d + p].astype(F32), lens)
        len_ref[i * 128 : (i + 1) * 128] = jnp.broadcast_to(lens, (128, 128))

    rp2.wait_recv()
    rp4.wait_recv()

    def finish_rows(base, one_slot, two_slot):
        def one(i, carry):
            at = pl.ds(pl.multiple_of(i * 128, 128), 128)
            there = pl.ds(pl.multiple_of(base + i * 128, 128), 128)
            value = own_sum[there] + rp_recv[one_slot, at].astype(F32) + rp_recv[two_slot, at].astype(F32)
            factor = rcol[there]
            kt[base // 128 + i] = (value[:, :HEAD] * factor).T.astype(BF16)
            vc[there] = (value[:, HEAD:] * factor).astype(BF16)
            return carry

        lax.fori_loop(0, HALF // 128, one, 0)

    finish_rows(0, 2, 4)
    rp3.wait_recv()
    rp5.wait_recv()
    finish_rows(HALF, 3, 5)

    wait_many(qr, QX)
    root = float(HEAD) ** -0.5
    rows3 = GROUP * 128

    def thrice(value):
        return jnp.concatenate([value] * GROUP, axis=0)

    def attend(step, carry):
        i = (z // 2 + step) % 4
        at = pl.ds(pl.multiple_of(i * 128, 128), 128)
        sources = pl.ds(pl.multiple_of(i * 8, 8), 8)
        rows = qr[sources].reshape(128, WIDTH)
        own_k = rows[:, GROUP * HEAD : GROUP * HEAD + HEAD]
        own_v = rows[:, GROUP * HEAD + HEAD :]
        pid = thrice(pid_ref[at, 0:1])
        lens = thrice(len_ref[at, 0:1])
        live = iota((rows3, LP), 1).astype(F32) < lens
        r, cc = iota((rows3, 128), 0) & 127, iota((rows3, 128), 1)
        usable = ((r >> 2) == (cc >> 2)) & ((cc & 3) <= (r & 3))
        query = jnp.concatenate([rows[:, h * HEAD : (h + 1) * HEAD] for h in range(GROUP)], axis=0)
        scores = None
        for p in range(PROMPTS):
            keys = jnp.concatenate([kt[2 * p], kt[2 * p + 1]], axis=1)
            found = nn(query, keys)
            scores = found if p == 0 else jnp.where(pid == float(p), found, scores)
        scores = jnp.where(live, scores * root, HUGE_NEGATIVE)
        top = jnp.max(scores, axis=1, keepdims=True)
        weights = jnp.where(live, jnp.exp(scores - top), 0.0)
        mass = jnp.sum(weights, axis=1, keepdims=True)
        blended = jnp.zeros((rows3, HEAD), F32)
        for p in range(PROMPTS):
            masked = jnp.where(pid == float(p), weights, 0.0).astype(BF16)
            blended = blended + nn(masked, vc[p * LP : (p + 1) * LP])
        own = jnp.where(usable, nt(query, own_k) * root, HUGE_NEGATIVE)
        own_top = jnp.max(own, axis=1, keepdims=True)
        own_weights = jnp.where(usable, jnp.exp(own - own_top), 0.0)
        own_mass = jnp.sum(own_weights, axis=1, keepdims=True)
        own_blended = nn(own_weights.astype(BF16), own_v)
        highest = jnp.maximum(top, own_top)
        one, two = jnp.exp(top - highest), jnp.exp(own_top - highest)
        numerator = blended * one + own_blended * two
        denominator = mass * one + own_mass * two
        result = (numerator / denominator).astype(BF16)
        result = jnp.concatenate([result[h * 128 : (h + 1) * 128] for h in range(GROUP)], axis=1)
        ro_[sources] = result.reshape(8, SLOTS, GROUP * HEAD)

        def give(k, carry):
            to = i * 8 + k

            @pl.when(to != d)
            def _():
                remote(ro_.at[to], rr.at[d], RX, (to, t)).start()

            return carry

        lax.fori_loop(0, 8, give, 0)
        return carry

    lax.fori_loop(0, 4, attend, 0)
    rr[d] = ro_[d]
    wait_many(rr, RX)

    take = jnp.where(iota((DR, n_slots), 1) == target_col, 1.0, 0.0).astype(BF16)
    ax[c] = nn(take, rr[...].reshape(n_slots, GROUP * HEAD)).astype(BF16)
    ax_copy = same(ax.at[c], core)
    for copy in l_wo:
        copy.wait()
    for copy in wo_copies:
        copy.wait_recv()
    ax_copy.wait_recv()

    def out_partial(j, row):
        b = (y + j) % NY
        at = pl.ds(row, DHALF)
        return nn(ax[c, at], wob[0, b]) + nn(ax[oc, at], wob[1, b])

    def out_send(n, j, row, extra, dev):
        value = out_partial(j, row)
        if extra is not None:
            value = value + rs_recv[extra].astype(F32)
        rs_send[n] = value.astype(BF16)
        return send(rs_send.at[n], rs_recv.at[n], dev)

    o0 = out_send(0, 2, 0, None, dn)
    o1 = out_send(1, 2, DHALF, None, up)
    o2 = out_send(2, 1, 0, None, up)
    o3 = out_send(3, 3, DHALF, None, dn)
    o0.wait_recv()
    o4 = out_send(4, 3, 0, 0, dn)
    o1.wait_recv()
    o5 = out_send(5, 1, DHALF, 1, up)
    own_a = out_partial(0, 0)
    o2.wait_recv()
    o4.wait_recv()
    own_a = own_a + rs_recv[2].astype(F32) + rs_recv[4].astype(F32)
    out_ref[: DHALF // 4] = own_a.reshape(DHALF // 4, 4, D).astype(BF16)
    own_b = out_partial(0, DHALF)
    o3.wait_recv()
    o5.wait_recv()
    own_b = own_b + rs_recv[3].astype(F32) + rs_recv[5].astype(F32)
    out_ref[DHALF // 4 :] = own_b.reshape(DHALF // 4, 4, D).astype(BF16)

    for copy in sent:
        copy.wait_send()
    for ref, n in ((ids, IDS), (qo, QX), (ro_, RX)):
        many(ref, ss.at[n]).wait()


def shards(
    prompt_states, prompt_lengths, decode_states, sample_owner, sample_local,
    norm_gain, kv_weight, q_weight, output_weight,
):
    vmem = pl.BlockSpec(memory_space=pltpu.VMEM)
    hbm = pl.BlockSpec(memory_space=pl.ANY)
    out = pl.pallas_call(
        kernel,
        out_shape=jax.ShapeDtypeStruct((DR // 4, 4, D), BF16),
        in_specs=[hbm, hbm, vmem, vmem, vmem, pl.BlockSpec(memory_space=pltpu.SMEM), hbm, hbm, hbm],
        out_specs=vmem,
        scratch_shapes=[
            pltpu.VMEM((DR // 4, 4, D), BF16),
            pltpu.VMEM((PR, D), BF16),
            pltpu.VMEM((NT, DR, D), BF16),
            pltpu.VMEM((NC, PR, D), BF16),
            pltpu.VMEM((NT, 16, 128), F32),
            pltpu.VMEM((NDP, 1, 128), F32),
            pltpu.VMEM((NT, D, GROUP * HEAD), BF16),
            pltpu.VMEM((NY, 2, NZ, SLICE, 2 * HEAD), BF16),
            pltpu.VMEM((NY, 2, NZ, SLICE, 2 * HEAD), BF16),
            pltpu.VMEM((NC, NY, GROUP * HEAD, D), BF16),
            pltpu.VMEM((6, HALF, 2 * HEAD), BF16),
            pltpu.VMEM((6, HALF, 2 * HEAD), BF16),
            pltpu.VMEM((PR, 2 * HEAD), F32),
            pltpu.VMEM((PR // 128, HEAD, 128), BF16),
            pltpu.VMEM((PR, HEAD), BF16),
            pltpu.VMEM((DR, WIDTH), F32),
            pltpu.VMEM((NDP, SLOTS, WIDTH), BF16),
            pltpu.VMEM((NDP, SLOTS, WIDTH), BF16),
            pltpu.VMEM((NDP, SLOTS, GROUP * HEAD), BF16),
            pltpu.VMEM((NDP, SLOTS, GROUP * HEAD), BF16),
            pltpu.VMEM((NC, DR, GROUP * HEAD), BF16),
            pltpu.VMEM((6, DHALF, D), BF16),
            pltpu.VMEM((6, DHALF, D), BF16),
            pltpu.VMEM((NDP * SLOTS, 128), F32),
            pltpu.VMEM((NDP * SLOTS, 128), F32),
            pltpu.VMEM((PR + DR, 128), F32),
            pltpu.SemaphoreType.DMA((N_SEM,)),
            pltpu.SemaphoreType.DMA((N_SEM,)),
            pltpu.SemaphoreType.DMA((9,)),
        ],
        compiler_params=pltpu.CompilerParams(
            collective_id=0, has_side_effects=True, vmem_limit_bytes=56 * 1024 * 1024
        ),
    )(
        decode_states,
        prompt_states.reshape(PR, D),
        norm_gain,
        sample_owner.reshape(1, 64),
        sample_local.reshape(1, 64),
        prompt_lengths,
        kv_weight.reshape(NY, 2, NZ, SLICE, 2 * HEAD),
        q_weight.reshape(NT, D, GROUP * HEAD),
        output_weight.reshape(GROUP * HEAD, MODEL_WIDTH),
    )
    return out


def solution(mesh):
    placed = (
        P("dp", None, "tensor"),
        P(),
        P("dp", None, "tensor"),
        P("dp", None),
        P("dp"),
        P("tensor"),
        P(None, "tensor", None),
        P(None, "tensor", None),
        P("tensor", None, None),
    )
    return jax.shard_map(
        shards, mesh=mesh, in_specs=placed, out_specs=P("dp", None, "tensor"), check_vma=False
    )
```

```python
import jax
import jax.numpy as jnp
from jax import lax
from jax.experimental import pallas as pl
from jax.experimental.pallas import tpu as pltpu
from jax.sharding import PartitionSpec as P

MESH = pl.DeviceIdType.MESH
F32 = jnp.float32
BF16 = jnp.bfloat16

MODEL_WIDTH = 5120
EPSILON = 1e-06
HUGE_NEGATIVE = -1e30

NX, NZ, NY, NC = 4, 8, 4, 2
NDP = NX * NZ
NT = NY * NC
D = 640
HEAD = 128
GROUP = 3
PROMPTS = 4
LP = 256
PR = PROMPTS * LP
HALF = PR // 2
DR = 256
DHALF = DR // 2
SLOTS = 16
WIDTH = GROUP * HEAD + 2 * HEAD

Z_ROWS, X_ROWS = 48, 224

IDS, QX, RX, LX = 0, 1, 2, 3
N_SEM = 160


def nn(a, b):
    return lax.dot_general(a, b, (((1,), (0,)), ((), ())), preferred_element_type=F32)


def nt(a, b):
    return lax.dot_general(a, b, (((1,), (1,)), ((), ())), preferred_element_type=F32)


def exact(a, b):
    return lax.dot_general(
        a, b, (((1,), (0,)), ((), ())), precision=lax.Precision.HIGHEST, preferred_element_type=F32
    )


def iota(shape, dim):
    return lax.broadcasted_iota(jnp.int32, shape, dim)


def kernel(
    decode_hbm, prompt_hbm, gain_hbm, owner_hbm, local_hbm, lengths_hbm,
    kv_hbm, q_hbm, wo_hbm,
    out_hbm,
    gain_ref, owner_ref, local_ref, lengths_ref, out_ref, dec_raw, prm_raw, dg, ps, sg, ids, qw, kvw, wt, wob,
    rp_send, rp_recv, own_sum, kt, vc, acc, pj, qo, qr, lo, lr, mine_ref, ro_, rr, ax, rs_send, rs_recv,
    pid_ref, len_ref, rcol,
    ss, rs, ls,
):
    d = lax.axis_index("dp")
    t = lax.axis_index("tensor")
    z, x = d // NX, d % NX
    y, c = t // NC, t % NC
    oc = 1 - c

    def at_y(j):
        return (d, ((y + j) % NY) * NC + c)

    def at_z(j):
        return (((z + j) % NZ) * NX + x, t)

    def at_x(j):
        return (z * NX + (x + j) % NX, t)

    core = (d, y * NC + oc)
    up, dn = at_y(1), at_y(NY - 1)

    def block_of(j):
        return ((y + j) % NY) * NC + c

    def remote(src, dst, n, dev):
        return pltpu.make_async_remote_copy(
            src_ref=src, dst_ref=dst, send_sem=ss.at[n], recv_sem=rs.at[n],
            device_id=dev, device_id_type=MESH,
        )

    sent = []

    def send(src, dst, dev):
        copy = remote(src, dst, 4 + len(sent), dev)
        copy.start()
        sent.append(copy)
        return copy

    def local_copy(src, dst, n):
        copy = pltpu.make_async_copy(src, dst, ls.at[n])
        copy.start()
        return copy

    def many(ref, sem):
        part = ref.at[pl.ds(0, NDP - 1)]
        return pltpu.make_async_copy(part, part, sem)

    def send_many(ref, to_ref, n, per_target):
        def one(k, carry):
            to = (d + k) % NDP
            remote(ref.at[to if per_target else d], to_ref.at[d], n, (to, t)).start()
            return carry

        lax.fori_loop(1, NDP, one, 0)

    def wait_many(to_ref, n):
        many(to_ref, rs.at[n]).wait()

    l_dec = local_copy(decode_hbm, dec_raw, 0)
    l_gain = local_copy(gain_hbm, gain_ref, 9)
    l_owner = local_copy(owner_hbm, owner_ref, 10)
    l_local = local_copy(local_hbm, local_ref, 11)
    l_prm = local_copy(prompt_hbm, prm_raw, 1)
    l_lengths = local_copy(lengths_hbm, lengths_ref, 12)

    barrier = pltpu.get_barrier_semaphore()
    for k in range(1, NT):
        pl.semaphore_signal(barrier, inc=1, device_id=(d, (t + k) % NT), device_id_type=MESH)

    def greet(k, carry):
        pl.semaphore_signal(barrier, inc=1, device_id=((d + k) % NDP, t), device_id_type=MESH)
        return carry

    lax.fori_loop(1, NDP, greet, 0)
    pl.semaphore_wait(barrier, NT - 1 + NDP - 1)

    z_rows = pl.ds(pl.multiple_of(z * Z_ROWS, 16), Z_ROWS)
    x_rows = pl.ds(pl.multiple_of(NZ * Z_ROWS + x * X_ROWS, 16), X_ROWS)

    def slices(j):
        return [
            send(kv_hbm.at[(y + j) % NY, rows], wt.at[NY - j, rows], at_y(j))
            for rows in (z_rows, x_rows)
        ]

    arrives = {2: slices(2), 1: slices(3), 3: slices(1)}

    l_dec.wait()
    l_gain.wait()
    gain = gain_ref[...].reshape(1, D)
    decode = dec_raw[...].astype(F32).reshape(DR, D)
    dg[t] = (decode * gain).astype(BF16)
    A, B = pl.ds(0, DHALF), pl.ds(DHALF, DHALF)

    def block(k, rows, dev):
        return send(dg.at[k, rows], dg.at[k, rows], dev)

    up_a = block(t, A, up)
    dn_b = block(t, B, dn)
    up_b = block(t, B, up)
    dn_a = block(t, A, dn)
    g_core = send(dg.at[t], dg.at[t], core)

    l_q = local_copy(q_hbm, qw, 3)
    l_kv = local_copy(kv_hbm, kvw, 2)
    l_wt = local_copy(kv_hbm.at[y], wt.at[0], 4)
    l_wo = []
    for b in range(NY):
        cols = pl.ds(pl.multiple_of((2 * b + c) * D, 128), D)
        l_wo.append(local_copy(wo_hbm.at[:, cols], wob.at[0, b], 5 + b))

    l_owner.wait()
    l_local.wait()
    mine = (owner_ref[...] * PROMPTS + local_ref[...]).astype(F32)
    ids[d] = jnp.concatenate([mine, jnp.full((1, 64), -1.0, F32)], axis=1)
    send_many(ids, ids, IDS, False)

    ones = jnp.ones((8, D), BF16)

    def squares(value):
        sq = value * value
        high = sq.astype(BF16)
        low = (sq - high.astype(F32)).astype(BF16)
        return nt(ones, high) + nt(ones, low)

    row8 = iota((8, 128), 0)
    parts = [jnp.zeros((8, 128), F32)]

    def prompt_block(i):
        value = prm_raw[i * 128 : (i + 1) * 128].astype(F32)
        ps[c, i * 128 : (i + 1) * 128] = (value * gain).astype(BF16)
        parts[0] = jnp.where(row8 == i, squares(value), parts[0])

    def same(ref, dev):
        return send(ref, ref, dev)

    def spread_slices(slot):
        for copy in arrives[slot]:
            copy.wait_recv()
        copies = [same(wt.at[slot, x_rows], at_x(k)) for k in (2, 1, 3)]
        copies += [same(wt.at[slot, z_rows], at_z(k)) for k in (4, 3, 5, 2, 6, 1, 7)]
        return copies

    l_prm.wait()
    for i in range(4):
        prompt_block(i)
    spread = {2: spread_slices(2)}
    for i in range(4, PR // 128):
        prompt_block(i)
    ps_copy = same(ps.at[c], core)
    sg[t, 0:8] = parts[0]
    part = jnp.zeros((8, 128), F32)
    for i in range(DR // 128):
        part = jnp.where(row8 == i, squares(decode[i * 128 : (i + 1) * 128]), part)
    sg[t, 8:16] = part
    sq = [same(sg.at[t], (d, (t + k) % NT)) for k in range(1, NT)]

    spread[1] = spread_slices(1)
    spread[3] = spread_slices(3)

    r256, c256 = iota((DR, DR), 0), iota((DR, DR), 1)
    owners = jnp.broadcast_to(owner_ref[...].astype(F32), (8, 64)).astype(BF16)
    expand = jnp.where(iota((64, DR), 0) == (iota((64, DR), 1) >> 2), 1.0, 0.0).astype(BF16)
    owner_row = nn(owners, expand)[0:1].astype(jnp.int32)
    expand = jnp.where((iota((DR, 64), 0) >> 2) == iota((DR, 64), 1), 1.0, 0.0).astype(BF16)
    owner_col = nt(expand, owners)[:, 0:1].astype(jnp.int32)
    alike = (owner_col == owner_row) & ((r256 & 3) == (c256 & 3))
    rank_row = jnp.sum(jnp.where(alike & (r256 < c256), 1, 0), axis=0, keepdims=True)
    rank_col = jnp.sum(jnp.where(alike & (c256 < r256), 1, 0), axis=1, keepdims=True)
    lane_row = iota((1, DR), 1)
    lane_col = iota((DR, 1), 0)
    target_row = owner_row * SLOTS + rank_row * 4 + (lane_row & 3)
    target_col = owner_col * SLOTS + rank_col * 4 + (lane_col & 3)
    n_slots = NDP * SLOTS

    below, above, opposite = block_of(NY - 1), block_of(1), block_of(2)
    up_a.wait_recv()
    up_fa = block(below, A, up)
    dn_b.wait_recv()
    dn_fb = block(above, B, dn)
    relays = [block(below, A, core), block(above, B, core)]
    up_b.wait_recv()
    relays.append(block(below, B, core))
    dn_a.wait_recv()
    relays.append(block(above, A, core))

    l_q.wait()
    l_kv.wait()

    def project(k, first=False):
        add_q = nn(dg[k], qw[k])
        add_kv = nn(dg[k], kvw[k // 2, pl.ds(pl.multiple_of(k % 2 * D, D), D)])
        if first:
            acc[:, : GROUP * HEAD] = add_q
            acc[:, GROUP * HEAD :] = add_kv
        else:
            acc[:, : GROUP * HEAD] += add_q
            acc[:, GROUP * HEAD :] += add_kv

    project(t, True)

    ps_copy.wait_recv()
    l_wt.wait()

    def partial(j, row, rows):
        return nn(ps[0, row : row + rows], wt[j, :D]) + nn(ps[1, row : row + rows], wt[j, D:])

    def rp(n, dev):
        return send(rp_send.at[n], rp_recv.at[n], dev)

    def slot_ready(slot):
        for copy in spread[slot]:
            copy.wait_recv()

    slot_ready(2)
    rp_send[0] = partial(2, 0, HALF).astype(BF16)
    rp0 = rp(0, dn)
    rp_send[1] = partial(2, HALF, HALF).astype(BF16)
    rp1 = rp(1, up)
    project(below)
    project(above)

    up_fa.wait_recv()
    relays.append(block(opposite, A, core))
    dn_fb.wait_recv()
    relays.append(block(opposite, B, core))

    slot_ready(1)
    rp_send[2] = partial(1, 0, HALF).astype(BF16)
    rp2 = rp(2, up)
    slot_ready(3)
    rp_send[3] = partial(3, HALF, HALF).astype(BF16)
    rp3 = rp(3, dn)

    project(opposite)
    g_core.wait_recv()
    project(block_of(0) + oc - c)
    for copy in relays:
        copy.wait_recv()
    for j in range(1, NY):
        project(block_of(j) + oc - c)

    for copy in sq:
        copy.wait_recv()
    total = sg[0]
    for k in range(1, NT):
        total = total + sg[k]
    factor = lax.rsqrt(total / MODEL_WIDTH + EPSILON)
    for i in range((PR + DR) // 128):
        rcol[i * 128 : (i + 1) * 128] = jnp.broadcast_to(factor[i : i + 1], (128, 128)).T

    scale = rcol[PR : PR + DR]
    for i in range(WIDTH // 128):
        pj[:, i * 128 : (i + 1) * 128] = (acc[:, i * 128 : (i + 1) * 128] * scale).astype(BF16)
    for i in range(4):
        rows = iota((n_slots // 4, DR), 0) + i * (n_slots // 4)
        pick = jnp.where(rows == target_row, 1.0, 0.0).astype(BF16)
        placed = nn(pick, pj[:, : GROUP * HEAD]).astype(BF16)
        qo[i * 8 : (i + 1) * 8] = placed.reshape(8, SLOTS, GROUP * HEAD)
    qr[d] = qo[d]
    send_many(qo, qr, QX, True)

    part = partial(3, 0, HALF)
    rp0.wait_recv()
    rp_send[4] = (part + rp_recv[0].astype(F32)).astype(BF16)
    rp4 = rp(4, dn)
    part = partial(1, HALF, HALF)
    rp1.wait_recv()
    rp_send[5] = (part + rp_recv[1].astype(F32)).astype(BF16)
    rp5 = rp(5, up)
    own_sum[:HALF] = partial(0, 0, HALF)
    own_sum[HALF:] = partial(0, HALF, HALF)

    wo_copies = []
    for b in range(NY):
        cols = pl.ds(pl.multiple_of((2 * b + oc) * D, 128), D)
        wo_copies.append(send(wo_hbm.at[:, cols], wob.at[1, b], core))

    root = float(HEAD) ** -0.5
    rows3 = GROUP * 128

    def heads_down(value):
        return jnp.concatenate([value[:, h * HEAD : (h + 1) * HEAD] for h in range(GROUP)], axis=0)

    def heads_across(value):
        return jnp.concatenate([value[h * 128 : (h + 1) * 128] for h in range(GROUP)], axis=1)

    for i in range(2):
        rows = pj[i * 128 : (i + 1) * 128]
        r, cc = iota((rows3, 128), 0) & 127, iota((rows3, 128), 1)
        usable = ((r >> 2) == (cc >> 2)) & ((cc & 3) <= (r & 3))
        query = heads_down(rows)
        own = nt(query, rows[:, GROUP * HEAD : GROUP * HEAD + HEAD]) * root
        own = jnp.where(usable, own, HUGE_NEGATIVE)
        own_top = jnp.max(own, axis=1, keepdims=True)
        own_weights = jnp.where(usable, jnp.exp(own - own_top), 0.0)
        own_mass = jnp.sum(own_weights, axis=1, keepdims=True)
        mine_ref[i, 0] = nn(own_weights.astype(BF16), rows[:, GROUP * HEAD + HEAD :])
        mine_ref[i, 1] = jnp.broadcast_to(own_top, (rows3, 128))
        mine_ref[i, 2] = jnp.broadcast_to(own_mass, (rows3, 128))

    l_lengths.wait()
    wait_many(ids, IDS)
    which = jnp.concatenate([ids[s] for s in range(NDP)], axis=0)
    local = which - (PROMPTS * d).astype(F32)
    match = (local >= 0.0) & (local < float(PROMPTS))
    before = jnp.where(iota((128, 128), 0) < iota((128, 128), 1), 1.0, 0.0).astype(BF16)
    rank = nn(jnp.where(match, 1.0, 0.0).astype(BF16), before)
    lane = iota((NDP, 128), 1)
    table = jnp.zeros((NDP, 128), F32)
    for k in range(4):
        at_k = jnp.sum(
            jnp.where(match & (rank == float(k)), local, 0.0), axis=1, keepdims=True
        )
        table = jnp.where(lane == k, at_k, table)
    table = table.astype(BF16)
    for i in range(4):
        sub = iota((128, NDP), 0)
        spread = jnp.where((sub >> 4) + 8 * i == iota((128, NDP), 1), 1.0, 0.0).astype(BF16)
        wide = nn(spread, table)
        mine = iota((128, 128), 1) == ((iota((128, 128), 0) >> 2) & 3)
        pid = jnp.sum(jnp.where(mine, wide, 0.0), axis=1, keepdims=True)
        pid_ref[i * 128 : (i + 1) * 128] = jnp.broadcast_to(pid, (128, 128))
        lens = jnp.zeros((128, 1), F32)
        for p in range(PROMPTS):
            lens = jnp.where(pid == float(p), lengths_ref[PROMPTS * d + p].astype(F32), lens)
        len_ref[i * 128 : (i + 1) * 128] = jnp.broadcast_to(lens, (128, 128))

    rp2.wait_recv()
    rp4.wait_recv()

    def finish_rows(base, one_slot, two_slot):
        def one(i, carry):
            at = pl.ds(pl.multiple_of(i * 128, 128), 128)
            there = pl.ds(pl.multiple_of(base + i * 128, 128), 128)
            value = own_sum[there] + rp_recv[one_slot, at].astype(F32) + rp_recv[two_slot, at].astype(F32)
            factor = rcol[there]
            kt[base // 128 + i] = (value[:, :HEAD] * factor).T.astype(BF16)
            vc[there] = (value[:, HEAD:] * factor).astype(BF16)
            return carry

        lax.fori_loop(0, HALF // 128, one, 0)

    finish_rows(0, 2, 4)
    rp3.wait_recv()
    rp5.wait_recv()
    finish_rows(HALF, 3, 5)

    wait_many(qr, QX)
    def thrice(value):
        return jnp.concatenate([value] * GROUP, axis=0)

    def attend(step, carry):
        i = (z // 2 + step) % 4
        at = pl.ds(pl.multiple_of(i * 128, 128), 128)
        sources = pl.ds(pl.multiple_of(i * 8, 8), 8)
        query = heads_down(qr[sources].reshape(128, GROUP * HEAD))
        pid = thrice(pid_ref[at, 0:1])
        lens = thrice(len_ref[at, 0:1])
        live = iota((rows3, LP), 1).astype(F32) < lens
        scores = None
        for p in range(PROMPTS):
            keys = jnp.concatenate([kt[2 * p], kt[2 * p + 1]], axis=1)
            found = nn(query, keys)
            scores = found if p == 0 else jnp.where(pid == float(p), found, scores)
        scores = jnp.where(live, scores * root, HUGE_NEGATIVE)
        top = jnp.max(scores, axis=1, keepdims=True)
        weights = jnp.where(live, jnp.exp(scores - top), 0.0)
        mass = jnp.sum(weights, axis=1, keepdims=True)
        blended = jnp.zeros((rows3, HEAD), F32)
        for p in range(PROMPTS):
            masked = jnp.where(pid == float(p), weights, 0.0).astype(BF16)
            blended = blended + nn(masked, vc[p * LP : (p + 1) * LP])
        result = heads_across((blended / mass).astype(BF16))
        ro_[sources] = result.reshape(8, SLOTS, GROUP * HEAD)
        level = top + jnp.log(mass)
        row, lane = iota((128, 128), 0), iota((128, 128), 1)
        wide = jnp.zeros((128, 128), F32)
        for h in range(GROUP):
            wide = jnp.where((lane >> 4) == h, level[h * 128 : (h + 1) * 128], wide)
        wide = jnp.where((lane & 15) == (row & 15), wide, 0.0)
        gather = jnp.where((iota((8, 128), 1) >> 4) == iota((8, 128), 0), 1.0, 0.0)
        levels = exact(gather, wide)
        for k in range(8):
            lo[i * 8 + k] = levels[k : k + 1]

        def give(k, carry):
            to = i * 8 + k

            @pl.when(to != d)
            def _():
                remote(ro_.at[to], rr.at[d], RX, (to, t)).start()
                remote(lo.at[to], lr.at[d], LX, (to, t)).start()

            return carry

        lax.fori_loop(0, 8, give, 0)
        return carry

    lax.fori_loop(0, 4, attend, 0)
    rr[d] = ro_[d]
    lr[d] = lo[d]
    wait_many(lr, LX)
    wait_many(rr, RX)

    levels = jnp.concatenate([lr[s] for s in range(NDP)], axis=0)
    prefix = rr[...].reshape(n_slots, GROUP * HEAD)
    for i in range(2):
        target = target_col[i * 128 : (i + 1) * 128]
        take = jnp.where(iota((128, n_slots), 1) == target, 1.0, 0.0).astype(BF16)
        found = heads_down(nn(take, prefix))
        owner = jnp.where(iota((128, NDP), 1) == (target >> 4), 1.0, 0.0)
        level = exact(owner, levels)
        lane = iota((128, 128), 1)
        level = jnp.concatenate(
            [
                jnp.sum(jnp.where(lane == h * 16 + (target & 15), level, 0.0), axis=1, keepdims=True)
                for h in range(GROUP)
            ],
            axis=0,
        )
        own_blended, own_top, own_mass = mine_ref[i, 0], mine_ref[i, 1], mine_ref[i, 2]
        highest = jnp.maximum(level, own_top)
        one, two = jnp.exp(level - highest), jnp.exp(own_top - highest)
        merged = (found * one + own_blended * two) / (one + own_mass * two)
        ax[c, i * 128 : (i + 1) * 128] = heads_across(merged.astype(BF16))
    ax_copy = same(ax.at[c], core)
    for copy in l_wo:
        copy.wait()
    for copy in wo_copies:
        copy.wait_recv()
    ax_copy.wait_recv()

    def out_partial(j, row):
        b = (y + j) % NY
        at = pl.ds(row, DHALF)
        return nn(ax[c, at], wob[0, b]) + nn(ax[oc, at], wob[1, b])

    def out_send(n, j, row, extra, dev):
        value = out_partial(j, row)
        if extra is not None:
            value = value + rs_recv[extra].astype(F32)
        rs_send[n] = value.astype(BF16)
        return send(rs_send.at[n], rs_recv.at[n], dev)

    o0 = out_send(0, 2, 0, None, dn)
    o1 = out_send(1, 2, DHALF, None, up)
    o2 = out_send(2, 1, 0, None, up)
    o3 = out_send(3, 3, DHALF, None, dn)
    o0.wait_recv()
    o4 = out_send(4, 3, 0, 0, dn)
    o1.wait_recv()
    o5 = out_send(5, 1, DHALF, 1, up)
    own_a = out_partial(0, 0)
    o2.wait_recv()
    o4.wait_recv()
    own_a = own_a + rs_recv[2].astype(F32) + rs_recv[4].astype(F32)
    out_ref[: DHALF // 4] = own_a.reshape(DHALF // 4, 4, D).astype(BF16)
    first, second = pl.ds(0, DHALF // 4), pl.ds(DHALF // 4, DHALF // 4)
    out_a = local_copy(out_ref.at[first], out_hbm.at[first], 13)
    own_b = out_partial(0, DHALF)
    o3.wait_recv()
    o5.wait_recv()
    own_b = own_b + rs_recv[3].astype(F32) + rs_recv[5].astype(F32)
    out_ref[DHALF // 4 :] = own_b.reshape(DHALF // 4, 4, D).astype(BF16)
    out_b = local_copy(out_ref.at[second], out_hbm.at[second], 14)

    out_a.wait()
    out_b.wait()
    for copy in sent:
        copy.wait_send()
    for ref, n in ((ids, IDS), (qo, QX), (ro_, RX), (lo, LX)):
        many(ref, ss.at[n]).wait()


def shards(
    prompt_states, prompt_lengths, decode_states, sample_owner, sample_local,
    norm_gain, kv_weight, q_weight, output_weight,
):
    hbm = pl.BlockSpec(memory_space=pl.ANY)
    out = pl.pallas_call(
        kernel,
        out_shape=jax.ShapeDtypeStruct((DR // 4, 4, D), BF16),
        in_specs=[hbm] * 9,
        out_specs=hbm,
        scratch_shapes=[
            pltpu.VMEM((D,), F32),
            pltpu.VMEM((1, 64), jnp.int32),
            pltpu.VMEM((1, 64), jnp.int32),
            pltpu.SMEM((NDP * PROMPTS,), jnp.int32),
            pltpu.VMEM((DR // 4, 4, D), BF16),
            pltpu.VMEM((DR // 4, 4, D), BF16),
            pltpu.VMEM((PR, D), BF16),
            pltpu.VMEM((NT, DR, D), BF16),
            pltpu.VMEM((NC, PR, D), BF16),
            pltpu.VMEM((NT, 16, 128), F32),
            pltpu.VMEM((NDP, 1, 128), F32),
            pltpu.VMEM((NT, D, GROUP * HEAD), BF16),
            pltpu.VMEM((NY, 2 * D, 2 * HEAD), BF16),
            pltpu.VMEM((NY, 2 * D, 2 * HEAD), BF16),
            pltpu.VMEM((NC, NY, GROUP * HEAD, D), BF16),
            pltpu.VMEM((6, HALF, 2 * HEAD), BF16),
            pltpu.VMEM((6, HALF, 2 * HEAD), BF16),
            pltpu.VMEM((PR, 2 * HEAD), F32),
            pltpu.VMEM((PR // 128, HEAD, 128), BF16),
            pltpu.VMEM((PR, HEAD), BF16),
            pltpu.VMEM((DR, WIDTH), F32),
            pltpu.VMEM((DR, WIDTH), BF16),
            pltpu.VMEM((NDP, SLOTS, GROUP * HEAD), BF16),
            pltpu.VMEM((NDP, SLOTS, GROUP * HEAD), BF16),
            pltpu.VMEM((NDP, 1, 128), F32),
            pltpu.VMEM((NDP, 1, 128), F32),
            pltpu.VMEM((2, 3, GROUP * 128, 128), F32),
            pltpu.VMEM((NDP, SLOTS, GROUP * HEAD), BF16),
            pltpu.VMEM((NDP, SLOTS, GROUP * HEAD), BF16),
            pltpu.VMEM((NC, DR, GROUP * HEAD), BF16),
            pltpu.VMEM((6, DHALF, D), BF16),
            pltpu.VMEM((6, DHALF, D), BF16),
            pltpu.VMEM((NDP * SLOTS, 128), F32),
            pltpu.VMEM((NDP * SLOTS, 128), F32),
            pltpu.VMEM((PR + DR, 128), F32),
            pltpu.SemaphoreType.DMA((N_SEM,)),
            pltpu.SemaphoreType.DMA((N_SEM,)),
            pltpu.SemaphoreType.DMA((15,)),
        ],
        compiler_params=pltpu.CompilerParams(
            collective_id=0, has_side_effects=True, vmem_limit_bytes=56 * 1024 * 1024
        ),
    )(
        decode_states,
        prompt_states.reshape(PR, D),
        norm_gain,
        sample_owner.reshape(1, 64),
        sample_local.reshape(1, 64),
        prompt_lengths,
        kv_weight.reshape(NY, 2 * D, 2 * HEAD),
        q_weight.reshape(NT, D, GROUP * HEAD),
        output_weight.reshape(GROUP * HEAD, MODEL_WIDTH),
    )
    return out


def solution(mesh):
    placed = (
        P("dp", None, "tensor"),
        P(),
        P("dp", None, "tensor"),
        P("dp", None),
        P("dp"),
        P("tensor"),
        P(None, "tensor", None),
        P(None, "tensor", None),
        P("tensor", None, None),
    )
    return jax.shard_map(
        shards, mesh=mesh, in_specs=placed, out_specs=P("dp", None, "tensor"), check_vma=False
    )
```

```python
import jax
import jax.numpy as jnp
from jax import lax
from jax.experimental import pallas as pl
from jax.experimental.pallas import tpu as pltpu
from jax.sharding import PartitionSpec as P

MESH = pl.DeviceIdType.MESH
F32 = jnp.float32
BF16 = jnp.bfloat16

MODEL_WIDTH = 5120
EPSILON = 1e-06
HUGE_NEGATIVE = -1e30

NX, NZ, NY, NC = 4, 8, 4, 2
NDP = NX * NZ
NT = NY * NC
D = 640
HEAD = 128
GROUP = 3
PROMPTS = 4
LP = 256
PR = PROMPTS * LP
HALF = PR // 2
DR = 256
DHALF = DR // 2
SLOTS = 16
WIDTH = GROUP * HEAD + 2 * HEAD

Z_ROWS, X_ROWS = 48, 224

IDS, QX, RX, LX = 0, 1, 2, 3
N_SEM = 160


def nn(a, b):
    return lax.dot_general(a, b, (((1,), (0,)), ((), ())), preferred_element_type=F32)


def nt(a, b):
    return lax.dot_general(a, b, (((1,), (1,)), ((), ())), preferred_element_type=F32)


def exact(a, b):
    return lax.dot_general(
        a, b, (((1,), (0,)), ((), ())), precision=lax.Precision.HIGHEST, preferred_element_type=F32
    )


def iota(shape, dim):
    return lax.broadcasted_iota(jnp.int32, shape, dim)


def kernel(
    decode_hbm, prompt_hbm, gain_hbm, owner_hbm, local_hbm, lengths_hbm,
    kv_hbm, q_hbm, wo_hbm,
    out_hbm,
    gain_ref, owner_ref, local_ref, lengths_ref, out_ref, dec_raw, prm_raw, dg, ps, sg, ids, qw, kvw, wt, wob,
    rp_send, rp_recv, own_sum, kt, vc, acc, pj, qo, qr, lo, lr, mine_ref, take_ref, ro_, rr, ax, rs_send, rs_recv,
    pid_ref, len_ref, rcol,
    ss, rs, ls,
):
    d = lax.axis_index("dp")
    t = lax.axis_index("tensor")
    z, x = d // NX, d % NX
    y, c = t // NC, t % NC
    oc = 1 - c

    def at_y(j):
        return (d, ((y + j) % NY) * NC + c)

    def at_z(j):
        return (((z + j) % NZ) * NX + x, t)

    def at_x(j):
        return (z * NX + (x + j) % NX, t)

    core = (d, y * NC + oc)
    up, dn = at_y(1), at_y(NY - 1)

    def block_of(j):
        return ((y + j) % NY) * NC + c

    def remote(src, dst, n, dev):
        return pltpu.make_async_remote_copy(
            src_ref=src, dst_ref=dst, send_sem=ss.at[n], recv_sem=rs.at[n],
            device_id=dev, device_id_type=MESH,
        )

    sent = []

    def send(src, dst, dev):
        copy = remote(src, dst, 4 + len(sent), dev)
        copy.start()
        sent.append(copy)
        return copy

    def local_copy(src, dst, n):
        copy = pltpu.make_async_copy(src, dst, ls.at[n])
        copy.start()
        return copy

    def many(ref, sem):
        part = ref.at[pl.ds(0, NDP - 1)]
        return pltpu.make_async_copy(part, part, sem)

    def send_many(ref, to_ref, n, per_target):
        def to_one(to):
            remote(ref.at[to if per_target else d], to_ref.at[d], n, (to, t)).start()

        def two(k, carry):
            to_one((d + NDP // 2 - k) % NDP)
            to_one((d + NDP // 2 + k) % NDP)
            return carry

        to_one((d + NDP // 2) % NDP)
        lax.fori_loop(1, NDP // 2, two, 0)

    def wait_many(to_ref, n):
        many(to_ref, rs.at[n]).wait()

    l_dec = local_copy(decode_hbm, dec_raw, 0)
    l_gain = local_copy(gain_hbm, gain_ref, 9)
    l_owner = local_copy(owner_hbm, owner_ref, 10)
    l_local = local_copy(local_hbm, local_ref, 11)
    l_prm = local_copy(prompt_hbm, prm_raw, 1)
    l_lengths = local_copy(lengths_hbm, lengths_ref, 12)

    barrier = pltpu.get_barrier_semaphore()
    for k in range(1, NT):
        pl.semaphore_signal(barrier, inc=1, device_id=(d, (t + k) % NT), device_id_type=MESH)

    def greet(k, carry):
        pl.semaphore_signal(barrier, inc=1, device_id=((d + k) % NDP, t), device_id_type=MESH)
        return carry

    lax.fori_loop(1, NDP, greet, 0)
    pl.semaphore_wait(barrier, NT - 1 + NDP - 1)

    z_rows = pl.ds(pl.multiple_of(z * Z_ROWS, 16), Z_ROWS)
    x_rows = pl.ds(pl.multiple_of(NZ * Z_ROWS + x * X_ROWS, 16), X_ROWS)

    def slices(j):
        return [
            send(kv_hbm.at[(y + j) % NY, rows], wt.at[NY - j, rows], at_y(j))
            for rows in (z_rows, x_rows)
        ]

    arrives = {2: slices(2), 1: slices(3), 3: slices(1)}

    l_dec.wait()
    l_gain.wait()
    gain = gain_ref[...].reshape(1, D)
    decode = dec_raw[...].astype(F32).reshape(DR, D)
    dg[t] = (decode * gain).astype(BF16)
    A, B = pl.ds(0, DHALF), pl.ds(DHALF, DHALF)

    def block(k, rows, dev):
        return send(dg.at[k, rows], dg.at[k, rows], dev)

    up_a = block(t, A, up)
    dn_b = block(t, B, dn)
    up_b = block(t, B, up)
    dn_a = block(t, A, dn)
    g_core = send(dg.at[t], dg.at[t], core)

    l_q = local_copy(q_hbm, qw, 3)
    l_kv = local_copy(kv_hbm, kvw, 2)
    l_wt = local_copy(kv_hbm.at[y], wt.at[0], 4)
    l_wo = []
    for b in range(NY):
        cols = pl.ds(pl.multiple_of((2 * b + c) * D, 128), D)
        l_wo.append(local_copy(wo_hbm.at[:, cols], wob.at[0, b], 5 + b))

    l_owner.wait()
    l_local.wait()
    mine = (owner_ref[...] * PROMPTS + local_ref[...]).astype(F32)
    ids[d] = jnp.concatenate([mine, jnp.full((1, 64), -1.0, F32)], axis=1)
    send_many(ids, ids, IDS, False)

    ones = jnp.ones((8, D), BF16)

    def squares(value):
        sq = value * value
        high = sq.astype(BF16)
        low = (sq - high.astype(F32)).astype(BF16)
        return nt(ones, high) + nt(ones, low)

    row8 = iota((8, 128), 0)
    parts = [jnp.zeros((8, 128), F32)]

    def prompt_block(i):
        value = prm_raw[i * 128 : (i + 1) * 128].astype(F32)
        ps[c, i * 128 : (i + 1) * 128] = (value * gain).astype(BF16)
        parts[0] = jnp.where(row8 == i, squares(value), parts[0])

    def same(ref, dev):
        return send(ref, ref, dev)

    def spread_slices(slot):
        for copy in arrives[slot]:
            copy.wait_recv()
        copies = [same(wt.at[slot, x_rows], at_x(k)) for k in (2, 1, 3)]
        copies += [same(wt.at[slot, z_rows], at_z(k)) for k in (4, 3, 5, 2, 6, 1, 7)]
        return copies

    l_prm.wait()
    for i in range(4):
        prompt_block(i)
    spread = {2: spread_slices(2)}
    for i in range(4, PR // 128):
        prompt_block(i)
    ps_copy = same(ps.at[c], core)
    sg[t, 0:8] = parts[0]
    part = jnp.zeros((8, 128), F32)
    for i in range(DR // 128):
        part = jnp.where(row8 == i, squares(decode[i * 128 : (i + 1) * 128]), part)
    sg[t, 8:16] = part
    sq = [same(sg.at[t], (d, (t + k) % NT)) for k in range(1, NT)]

    spread[1] = spread_slices(1)
    spread[3] = spread_slices(3)

    r256, c256 = iota((DR, DR), 0), iota((DR, DR), 1)
    owners = jnp.broadcast_to(owner_ref[...].astype(F32), (8, 64)).astype(BF16)
    expand = jnp.where(iota((64, DR), 0) == (iota((64, DR), 1) >> 2), 1.0, 0.0).astype(BF16)
    owner_row = nn(owners, expand)[0:1].astype(jnp.int32)
    expand = jnp.where((iota((DR, 64), 0) >> 2) == iota((DR, 64), 1), 1.0, 0.0).astype(BF16)
    owner_col = nt(expand, owners)[:, 0:1].astype(jnp.int32)
    alike = (owner_col == owner_row) & ((r256 & 3) == (c256 & 3))
    rank_row = jnp.sum(jnp.where(alike & (r256 < c256), 1, 0), axis=0, keepdims=True)
    rank_col = jnp.sum(jnp.where(alike & (c256 < r256), 1, 0), axis=1, keepdims=True)
    lane_row = iota((1, DR), 1)
    lane_col = iota((DR, 1), 0)
    target_row = owner_row * SLOTS + rank_row * 4 + (lane_row & 3)
    target_col = owner_col * SLOTS + rank_col * 4 + (lane_col & 3)
    n_slots = NDP * SLOTS

    below, above, opposite = block_of(NY - 1), block_of(1), block_of(2)
    up_a.wait_recv()
    up_fa = block(below, A, up)
    dn_b.wait_recv()
    dn_fb = block(above, B, dn)
    relays = [block(below, A, core), block(above, B, core)]
    up_b.wait_recv()
    relays.append(block(below, B, core))
    dn_a.wait_recv()
    relays.append(block(above, A, core))

    l_q.wait()
    l_kv.wait()

    def project(k, first=False):
        add_q = nn(dg[k], qw[k])
        add_kv = nn(dg[k], kvw[k // 2, pl.ds(pl.multiple_of(k % 2 * D, D), D)])
        if first:
            acc[:, : GROUP * HEAD] = add_q
            acc[:, GROUP * HEAD :] = add_kv
        else:
            acc[:, : GROUP * HEAD] += add_q
            acc[:, GROUP * HEAD :] += add_kv

    project(t, True)

    ps_copy.wait_recv()
    l_wt.wait()

    def partial(j, row, rows):
        return nn(ps[0, row : row + rows], wt[j, :D]) + nn(ps[1, row : row + rows], wt[j, D:])

    def rp(n, dev):
        return send(rp_send.at[n], rp_recv.at[n], dev)

    def slot_ready(slot):
        for copy in spread[slot]:
            copy.wait_recv()

    slot_ready(2)
    rp_send[0] = partial(2, 0, HALF).astype(BF16)
    rp0 = rp(0, dn)
    rp_send[1] = partial(2, HALF, HALF).astype(BF16)
    rp1 = rp(1, up)
    project(below)
    project(above)

    up_fa.wait_recv()
    relays.append(block(opposite, A, core))
    dn_fb.wait_recv()
    relays.append(block(opposite, B, core))

    slot_ready(1)
    rp_send[2] = partial(1, 0, HALF).astype(BF16)
    rp2 = rp(2, up)
    slot_ready(3)
    rp_send[3] = partial(3, HALF, HALF).astype(BF16)
    rp3 = rp(3, dn)

    project(opposite)
    g_core.wait_recv()
    project(block_of(0) + oc - c)
    for copy in relays:
        copy.wait_recv()
    for j in range(1, NY):
        project(block_of(j) + oc - c)

    for copy in sq:
        copy.wait_recv()
    total = sg[0]
    for k in range(1, NT):
        total = total + sg[k]
    factor = lax.rsqrt(total / MODEL_WIDTH + EPSILON)
    for i in range((PR + DR) // 128):
        rcol[i * 128 : (i + 1) * 128] = jnp.broadcast_to(factor[i : i + 1], (128, 128)).T

    scale = rcol[PR : PR + DR]
    for i in range(WIDTH // 128):
        pj[:, i * 128 : (i + 1) * 128] = (acc[:, i * 128 : (i + 1) * 128] * scale).astype(BF16)
    for i in range(4):
        rows = iota((n_slots // 4, DR), 0) + i * (n_slots // 4)
        pick = jnp.where(rows == target_row, 1.0, 0.0).astype(BF16)
        placed = nn(pick, pj[:, : GROUP * HEAD]).astype(BF16)
        qo[i * 8 : (i + 1) * 8] = placed.reshape(8, SLOTS, GROUP * HEAD)
    qr[d] = qo[d]
    send_many(qo, qr, QX, True)

    part = partial(3, 0, HALF)
    rp0.wait_recv()
    rp_send[4] = (part + rp_recv[0].astype(F32)).astype(BF16)
    rp4 = rp(4, dn)
    part = partial(1, HALF, HALF)
    rp1.wait_recv()
    rp_send[5] = (part + rp_recv[1].astype(F32)).astype(BF16)
    rp5 = rp(5, up)
    own_sum[:HALF] = partial(0, 0, HALF)
    own_sum[HALF:] = partial(0, HALF, HALF)

    wo_copies = []
    for b in range(NY):
        cols = pl.ds(pl.multiple_of((2 * b + oc) * D, 128), D)
        wo_copies.append(send(wo_hbm.at[:, cols], wob.at[1, b], core))

    root = float(HEAD) ** -0.5
    rows3 = GROUP * 128

    def heads_down(value):
        return jnp.concatenate([value[:, h * HEAD : (h + 1) * HEAD] for h in range(GROUP)], axis=0)

    def heads_across(value):
        return jnp.concatenate([value[h * 128 : (h + 1) * 128] for h in range(GROUP)], axis=1)

    for i in range(2):
        rows = pj[i * 128 : (i + 1) * 128]
        r, cc = iota((rows3, 128), 0) & 127, iota((rows3, 128), 1)
        usable = ((r >> 2) == (cc >> 2)) & ((cc & 3) <= (r & 3))
        query = heads_down(rows)
        own = nt(query, rows[:, GROUP * HEAD : GROUP * HEAD + HEAD]) * root
        own = jnp.where(usable, own, HUGE_NEGATIVE)
        own_top = jnp.max(own, axis=1, keepdims=True)
        own_weights = jnp.where(usable, jnp.exp(own - own_top), 0.0)
        own_mass = jnp.sum(own_weights, axis=1, keepdims=True)
        mine_ref[i, 0] = nn(own_weights.astype(BF16), rows[:, GROUP * HEAD + HEAD :])
        mine_ref[i, 1] = jnp.broadcast_to(own_top, (rows3, 128))
        mine_ref[i, 2] = jnp.broadcast_to(own_mass, (rows3, 128))

    l_lengths.wait()
    wait_many(ids, IDS)
    which = jnp.concatenate([ids[s] for s in range(NDP)], axis=0)
    local = which - (PROMPTS * d).astype(F32)
    match = (local >= 0.0) & (local < float(PROMPTS))
    before = jnp.where(iota((128, 128), 0) < iota((128, 128), 1), 1.0, 0.0).astype(BF16)
    rank = nn(jnp.where(match, 1.0, 0.0).astype(BF16), before)
    lane = iota((NDP, 128), 1)
    table = jnp.zeros((NDP, 128), F32)
    for k in range(4):
        at_k = jnp.sum(
            jnp.where(match & (rank == float(k)), local, 0.0), axis=1, keepdims=True
        )
        table = jnp.where(lane == k, at_k, table)
    table = table.astype(BF16)
    for i in range(4):
        sub = iota((128, NDP), 0)
        spread = jnp.where((sub >> 4) + 8 * i == iota((128, NDP), 1), 1.0, 0.0).astype(BF16)
        wide = nn(spread, table)
        mine = iota((128, 128), 1) == ((iota((128, 128), 0) >> 2) & 3)
        pid = jnp.sum(jnp.where(mine, wide, 0.0), axis=1, keepdims=True)
        pid_ref[i * 128 : (i + 1) * 128] = jnp.broadcast_to(pid, (128, 128))
        lens = jnp.zeros((128, 1), F32)
        for p in range(PROMPTS):
            lens = jnp.where(pid == float(p), lengths_ref[PROMPTS * d + p].astype(F32), lens)
        len_ref[i * 128 : (i + 1) * 128] = jnp.broadcast_to(lens, (128, 128))

    rp2.wait_recv()
    rp4.wait_recv()

    def finish_rows(base, one_slot, two_slot):
        def one(i, carry):
            at = pl.ds(pl.multiple_of(i * 128, 128), 128)
            there = pl.ds(pl.multiple_of(base + i * 128, 128), 128)
            value = own_sum[there] + rp_recv[one_slot, at].astype(F32) + rp_recv[two_slot, at].astype(F32)
            factor = rcol[there]
            kt[base // 128 + i] = (value[:, :HEAD] * factor).astype(BF16).T
            vc[there] = (value[:, HEAD:] * factor).astype(BF16)
            return carry

        lax.fori_loop(0, HALF // 128, one, 0)

    finish_rows(0, 2, 4)
    rp3.wait_recv()
    rp5.wait_recv()
    finish_rows(HALF, 3, 5)

    wait_many(qr, QX)
    def thrice(value):
        return jnp.concatenate([value] * GROUP, axis=0)

    def attend(step, carry):
        away = 4 - step
        planes = [(z + away) % NZ, (z + NZ - away - 4 * (away // 4)) % NZ]
        four = [pl.ds(pl.multiple_of(plane * NX, NX), NX) for plane in planes]
        at = [pl.ds(pl.multiple_of(plane * 64, 64), 64) for plane in planes]

        def both(ref):
            return jnp.concatenate([ref[rows, 0:1] for rows in at], axis=0)

        query = jnp.concatenate([qr[s].reshape(64, GROUP * HEAD) for s in four], axis=0)
        query = heads_down(query)
        pid = thrice(both(pid_ref))
        lens = thrice(both(len_ref))
        live = iota((rows3, LP), 1).astype(F32) < lens
        scores = None
        for p in range(PROMPTS):
            keys = jnp.concatenate([kt[2 * p], kt[2 * p + 1]], axis=1)
            found = nn(query, keys)
            scores = found if p == 0 else jnp.where(pid == float(p), found, scores)
        scores = jnp.where(live, scores * root, HUGE_NEGATIVE)
        top = jnp.max(scores, axis=1, keepdims=True)
        weights = jnp.where(live, jnp.exp(scores - top), 0.0)
        mass = jnp.sum(weights, axis=1, keepdims=True)
        blended = jnp.zeros((rows3, HEAD), F32)
        for p in range(PROMPTS):
            masked = jnp.where(pid == float(p), weights, 0.0).astype(BF16)
            blended = blended + nn(masked, vc[p * LP : (p + 1) * LP])
        result = heads_across((blended / mass).astype(BF16))
        for n in range(2):
            ro_[four[n]] = result[n * 64 : (n + 1) * 64].reshape(NX, SLOTS, GROUP * HEAD)
        level = top + jnp.log(mass)
        row, lane = iota((128, 128), 0), iota((128, 128), 1)
        wide = jnp.zeros((128, 128), F32)
        for h in range(GROUP):
            wide = jnp.where((lane >> 4) == h, level[h * 128 : (h + 1) * 128], wide)
        wide = jnp.where((lane & 15) == (row & 15), wide, 0.0)
        gather = jnp.where((iota((8, 128), 1) >> 4) == iota((8, 128), 0), 1.0, 0.0)
        levels = exact(gather, wide)
        for k in range(8):
            lo[planes[k // 4] * NX + k % 4] = levels[k : k + 1]

        def give(k, carry):
            to = ((z + away) * (1 - k % 2) + (z + NZ - away - 4 * (away // 4)) * (k % 2)) % NZ * NX + k // 2

            @pl.when(to != d)
            def _():
                remote(ro_.at[to], rr.at[d], RX, (to, t)).start()
                remote(lo.at[to], lr.at[d], LX, (to, t)).start()

            return carry

        lax.fori_loop(0, 8, give, 0)
        return carry

    lax.fori_loop(0, 4, attend, 0)
    rr[d] = ro_[d]
    lr[d] = lo[d]
    for i in range(2):
        rows = pl.ds(i * 128, 128)
        target = target_col[i * 128 : (i + 1) * 128]
        take_ref[rows] = jnp.where(iota((128, n_slots), 1) == target, 1.0, 0.0).astype(BF16)
    wait_many(lr, LX)
    wait_many(rr, RX)

    for copy in l_wo:
        copy.wait()
    for copy in wo_copies:
        copy.wait_recv()
    levels = jnp.concatenate([lr[s] for s in range(NDP)], axis=0)
    ax_copies = []
    prefix = rr[...].reshape(n_slots, GROUP * HEAD)
    for i in range(2):
        target = target_col[i * 128 : (i + 1) * 128]
        found = heads_down(nn(take_ref[i * 128 : (i + 1) * 128], prefix))
        owner = jnp.where(iota((128, NDP), 1) == (target >> 4), 1.0, 0.0)
        level = exact(owner, levels)
        lane = iota((128, 128), 1)
        level = jnp.concatenate(
            [
                jnp.sum(jnp.where(lane == h * 16 + (target & 15), level, 0.0), axis=1, keepdims=True)
                for h in range(GROUP)
            ],
            axis=0,
        )
        own_blended, own_top, own_mass = mine_ref[i, 0], mine_ref[i, 1], mine_ref[i, 2]
        highest = jnp.maximum(level, own_top)
        one, two = jnp.exp(level - highest), jnp.exp(own_top - highest)
        merged = (found * one + own_blended * two) / (one + own_mass * two)
        ax[c, i * 128 : (i + 1) * 128] = heads_across(merged.astype(BF16))
        ax_copies.append(same(ax.at[c, pl.ds(i * 128, 128)], core))

    def out_partial(j, row):
        b = (y + j) % NY
        at = pl.ds(row, DHALF)
        return nn(ax[c, at], wob[0, b]) + nn(ax[oc, at], wob[1, b])

    def out_send(n, j, row, extra, dev):
        value = out_partial(j, row)
        if extra is not None:
            value = value + rs_recv[extra].astype(F32)
        rs_send[n] = value.astype(BF16)
        return send(rs_send.at[n], rs_recv.at[n], dev)

    ax_copies[0].wait_recv()
    o0 = out_send(0, 2, 0, None, dn)
    ax_copies[1].wait_recv()
    o1 = out_send(1, 2, DHALF, None, up)
    o2 = out_send(2, 1, 0, None, up)
    o3 = out_send(3, 3, DHALF, None, dn)
    o0.wait_recv()
    o4 = out_send(4, 3, 0, 0, dn)
    o1.wait_recv()
    o5 = out_send(5, 1, DHALF, 1, up)
    own_a = out_partial(0, 0)
    o2.wait_recv()
    o4.wait_recv()
    own_a = own_a + rs_recv[2].astype(F32) + rs_recv[4].astype(F32)
    out_ref[: DHALF // 4] = own_a.reshape(DHALF // 4, 4, D).astype(BF16)
    first, second = pl.ds(0, DHALF // 4), pl.ds(DHALF // 4, DHALF // 4)
    out_a = local_copy(out_ref.at[first], out_hbm.at[first], 13)
    own_b = out_partial(0, DHALF)
    o3.wait_recv()
    o5.wait_recv()
    own_b = own_b + rs_recv[3].astype(F32) + rs_recv[5].astype(F32)
    out_ref[DHALF // 4 :] = own_b.reshape(DHALF // 4, 4, D).astype(BF16)
    out_b = local_copy(out_ref.at[second], out_hbm.at[second], 14)

    out_a.wait()
    out_b.wait()
    for copy in sent:
        copy.wait_send()
    for ref, n in ((ids, IDS), (qo, QX), (ro_, RX), (lo, LX)):
        many(ref, ss.at[n]).wait()


def shards(
    prompt_states, prompt_lengths, decode_states, sample_owner, sample_local,
    norm_gain, kv_weight, q_weight, output_weight,
):
    hbm = pl.BlockSpec(memory_space=pl.ANY)
    out = pl.pallas_call(
        kernel,
        out_shape=jax.ShapeDtypeStruct((DR // 4, 4, D), BF16),
        in_specs=[hbm] * 9,
        out_specs=hbm,
        scratch_shapes=[
            pltpu.VMEM((D,), F32),
            pltpu.VMEM((1, 64), jnp.int32),
            pltpu.VMEM((1, 64), jnp.int32),
            pltpu.SMEM((NDP * PROMPTS,), jnp.int32),
            pltpu.VMEM((DR // 4, 4, D), BF16),
            pltpu.VMEM((DR // 4, 4, D), BF16),
            pltpu.VMEM((PR, D), BF16),
            pltpu.VMEM((NT, DR, D), BF16),
            pltpu.VMEM((NC, PR, D), BF16),
            pltpu.VMEM((NT, 16, 128), F32),
            pltpu.VMEM((NDP, 1, 128), F32),
            pltpu.VMEM((NT, D, GROUP * HEAD), BF16),
            pltpu.VMEM((NY, 2 * D, 2 * HEAD), BF16),
            pltpu.VMEM((NY, 2 * D, 2 * HEAD), BF16),
            pltpu.VMEM((NC, NY, GROUP * HEAD, D), BF16),
            pltpu.VMEM((6, HALF, 2 * HEAD), BF16),
            pltpu.VMEM((6, HALF, 2 * HEAD), BF16),
            pltpu.VMEM((PR, 2 * HEAD), F32),
            pltpu.VMEM((PR // 128, HEAD, 128), BF16),
            pltpu.VMEM((PR, HEAD), BF16),
            pltpu.VMEM((DR, WIDTH), F32),
            pltpu.VMEM((DR, WIDTH), BF16),
            pltpu.VMEM((NDP, SLOTS, GROUP * HEAD), BF16),
            pltpu.VMEM((NDP, SLOTS, GROUP * HEAD), BF16),
            pltpu.VMEM((NDP, 1, 128), F32),
            pltpu.VMEM((NDP, 1, 128), F32),
            pltpu.VMEM((2, 3, GROUP * 128, 128), F32),
            pltpu.VMEM((DR, NDP * SLOTS), BF16),
            pltpu.VMEM((NDP, SLOTS, GROUP * HEAD), BF16),
            pltpu.VMEM((NDP, SLOTS, GROUP * HEAD), BF16),
            pltpu.VMEM((NC, DR, GROUP * HEAD), BF16),
            pltpu.VMEM((6, DHALF, D), BF16),
            pltpu.VMEM((6, DHALF, D), BF16),
            pltpu.VMEM((NDP * SLOTS, 128), F32),
            pltpu.VMEM((NDP * SLOTS, 128), F32),
            pltpu.VMEM((PR + DR, 128), F32),
            pltpu.SemaphoreType.DMA((N_SEM,)),
            pltpu.SemaphoreType.DMA((N_SEM,)),
            pltpu.SemaphoreType.DMA((15,)),
        ],
        compiler_params=pltpu.CompilerParams(
            collective_id=0, has_side_effects=True, vmem_limit_bytes=56 * 1024 * 1024
        ),
    )(
        decode_states,
        prompt_states.reshape(PR, D),
        norm_gain,
        sample_owner.reshape(1, 64),
        sample_local.reshape(1, 64),
        prompt_lengths,
        kv_weight.reshape(NY, 2 * D, 2 * HEAD),
        q_weight.reshape(NT, D, GROUP * HEAD),
        output_weight.reshape(GROUP * HEAD, MODEL_WIDTH),
    )
    return out


def solution(mesh):
    placed = (
        P("dp", None, "tensor"),
        P(),
        P("dp", None, "tensor"),
        P("dp", None),
        P("dp"),
        P("tensor"),
        P(None, "tensor", None),
        P(None, "tensor", None),
        P("tensor", None, None),
    )
    return jax.shard_map(
        shards, mesh=mesh, in_specs=placed, out_specs=P("dp", None, "tensor"), check_vma=False
    )
```

```python
import jax
import jax.numpy as jnp
from jax import lax
from jax.experimental import pallas as pl
from jax.experimental.pallas import tpu as pltpu
from jax.sharding import PartitionSpec as P

MESH = pl.DeviceIdType.MESH
F32 = jnp.float32
BF16 = jnp.bfloat16

MODEL_WIDTH = 5120
EPSILON = 1e-06
HUGE_NEGATIVE = -1e30

NX, NZ, NY, NC = 4, 8, 4, 2
NDP = NX * NZ
NT = NY * NC
D = 640
HEAD = 128
GROUP = 3
PROMPTS = 4
LP = 256
PR = PROMPTS * LP
HALF = PR // 2
DR = 256
DHALF = DR // 2
SLOTS = 16
WIDTH = GROUP * HEAD + 2 * HEAD

Z_ROWS, X_ROWS = 48, 224

IDS, QX, RX, LX = 0, 1, 2, 3
N_SEM = 160


def nn(a, b):
    return lax.dot_general(a, b, (((1,), (0,)), ((), ())), preferred_element_type=F32)


def nt(a, b):
    return lax.dot_general(a, b, (((1,), (1,)), ((), ())), preferred_element_type=F32)


def exact(a, b):
    return lax.dot_general(
        a, b, (((1,), (0,)), ((), ())), precision=lax.Precision.HIGHEST, preferred_element_type=F32
    )


def iota(shape, dim):
    return lax.broadcasted_iota(jnp.int32, shape, dim)


def kernel(
    decode_hbm, prompt_hbm, gain_hbm, owner_hbm, local_hbm, lengths_hbm,
    kv_hbm, q_hbm, wo_hbm,
    out_hbm,
    gain_ref, owner_ref, local_ref, lengths_ref, out_ref, dec_raw, prm_raw, dg, ps, sg, ids, qw, kvw, wt, wob,
    rp_send, rp_recv, own_sum, kt, vc, acc, pj, qo, qr, lo, lr, mine_ref, take_ref, ro_, rr, ax, rs_send, rs_recv,
    pid_ref, len_ref, rcol,
    ss, rs, ls,
):
    d = lax.axis_index("dp")
    t = lax.axis_index("tensor")
    z, x = d // NX, d % NX
    y, c = t // NC, t % NC
    oc = 1 - c

    def at_y(j):
        return (d, ((y + j) % NY) * NC + c)

    def at_z(j):
        return (((z + j) % NZ) * NX + x, t)

    def at_x(j):
        return (z * NX + (x + j) % NX, t)

    core = (d, y * NC + oc)
    up, dn = at_y(1), at_y(NY - 1)

    def block_of(j):
        return ((y + j) % NY) * NC + c

    def remote(src, dst, n, dev):
        return pltpu.make_async_remote_copy(
            src_ref=src, dst_ref=dst, send_sem=ss.at[n], recv_sem=rs.at[n],
            device_id=dev, device_id_type=MESH,
        )

    sent = []

    def send(src, dst, dev):
        copy = remote(src, dst, 4 + len(sent), dev)
        copy.start()
        sent.append(copy)
        return copy

    def local_copy(src, dst, n):
        copy = pltpu.make_async_copy(src, dst, ls.at[n])
        copy.start()
        return copy

    def many(ref, sem):
        part = ref.at[pl.ds(0, NDP - 1)]
        return pltpu.make_async_copy(part, part, sem)

    def send_many(ref, to_ref, n, per_target):
        def to_one(to):
            remote(ref.at[to if per_target else d], to_ref.at[d], n, (to, t)).start()

        def two(k, carry):
            to_one((d + NDP // 2 - k) % NDP)
            to_one((d + NDP // 2 + k) % NDP)
            return carry

        to_one((d + NDP // 2) % NDP)
        lax.fori_loop(1, NDP // 2, two, 0)

    def wait_many(to_ref, n):
        many(to_ref, rs.at[n]).wait()

    l_dec = local_copy(decode_hbm, dec_raw, 0)
    l_gain = local_copy(gain_hbm, gain_ref, 9)
    l_owner = local_copy(owner_hbm, owner_ref, 10)
    l_local = local_copy(local_hbm, local_ref, 11)
    l_prm = local_copy(prompt_hbm, prm_raw, 1)
    l_lengths = local_copy(lengths_hbm, lengths_ref, 12)

    barrier = pltpu.get_barrier_semaphore()
    for k in range(1, NT):
        pl.semaphore_signal(barrier, inc=1, device_id=(d, (t + k) % NT), device_id_type=MESH)

    def greet(k, carry):
        pl.semaphore_signal(barrier, inc=1, device_id=((d + k) % NDP, t), device_id_type=MESH)
        return carry

    lax.fori_loop(1, NDP, greet, 0)
    pl.semaphore_wait(barrier, NT - 1 + NDP - 1)

    z_rows = pl.ds(pl.multiple_of(z * Z_ROWS, 16), Z_ROWS)
    x_rows = pl.ds(pl.multiple_of(NZ * Z_ROWS + x * X_ROWS, 16), X_ROWS)

    def slices(j):
        return [
            send(kv_hbm.at[(y + j) % NY, rows], wt.at[NY - j, rows], at_y(j))
            for rows in (z_rows, x_rows)
        ]

    arrives = {2: slices(2), 1: slices(3), 3: slices(1)}

    l_dec.wait()
    l_gain.wait()
    gain = gain_ref[...].reshape(1, D)
    decode = dec_raw[...].astype(F32).reshape(DR, D)
    dg[t] = (decode * gain).astype(BF16)
    A, B = pl.ds(0, DHALF), pl.ds(DHALF, DHALF)

    def block(k, rows, dev):
        return send(dg.at[k, rows], dg.at[k, rows], dev)

    up_a = block(t, A, up)
    dn_b = block(t, B, dn)
    up_b = block(t, B, up)
    dn_a = block(t, A, dn)
    g_core = send(dg.at[t], dg.at[t], core)

    l_q = local_copy(q_hbm, qw, 3)
    l_kv = local_copy(kv_hbm, kvw, 2)
    l_wt = local_copy(kv_hbm.at[y], wt.at[0], 4)
    l_wo = []
    for b in range(NY):
        cols = pl.ds(pl.multiple_of((2 * b + c) * D, 128), D)
        l_wo.append(local_copy(wo_hbm.at[:, cols], wob.at[0, b], 5 + b))

    l_owner.wait()
    l_local.wait()
    mine = (owner_ref[...] * PROMPTS + local_ref[...]).astype(F32)
    ids[d] = jnp.concatenate([mine, jnp.full((1, 64), -1.0, F32)], axis=1)
    send_many(ids, ids, IDS, False)

    ones = jnp.ones((8, D), BF16)

    def squares(value):
        sq = value * value
        high = sq.astype(BF16)
        low = (sq - high.astype(F32)).astype(BF16)
        return nt(ones, high) + nt(ones, low)

    row8 = iota((8, 128), 0)
    parts = [jnp.zeros((8, 128), F32)]

    def prompt_block(i):
        value = prm_raw[i * 128 : (i + 1) * 128].astype(F32)
        ps[c, i * 128 : (i + 1) * 128] = (value * gain).astype(BF16)
        parts[0] = jnp.where(row8 == i, squares(value), parts[0])

    def same(ref, dev):
        return send(ref, ref, dev)

    def spread_slices(slot):
        for copy in arrives[slot]:
            copy.wait_recv()
        copies = [same(wt.at[slot, x_rows], at_x(k)) for k in (2, 1, 3)]
        copies += [same(wt.at[slot, z_rows], at_z(k)) for k in (4, 3, 5, 2, 6, 1, 7)]
        return copies

    l_prm.wait()
    for i in range(4):
        prompt_block(i)
    spread = {2: spread_slices(2)}
    for i in range(4, PR // 128):
        prompt_block(i)
    ps_copy = same(ps.at[c], core)
    sg[t, 0:8] = parts[0]
    part = jnp.zeros((8, 128), F32)
    for i in range(DR // 128):
        part = jnp.where(row8 == i, squares(decode[i * 128 : (i + 1) * 128]), part)
    sg[t, 8:16] = part
    sq = [same(sg.at[t], (d, (t + k) % NT)) for k in range(1, NT)]

    spread[1] = spread_slices(1)
    spread[3] = spread_slices(3)

    r256, c256 = iota((DR, DR), 0), iota((DR, DR), 1)
    owners = jnp.broadcast_to(owner_ref[...].astype(F32), (8, 64)).astype(BF16)
    expand = jnp.where(iota((64, DR), 0) == (iota((64, DR), 1) >> 2), 1.0, 0.0).astype(BF16)
    owner_row = nn(owners, expand)[0:1].astype(jnp.int32)
    expand = jnp.where((iota((DR, 64), 0) >> 2) == iota((DR, 64), 1), 1.0, 0.0).astype(BF16)
    owner_col = nt(expand, owners)[:, 0:1].astype(jnp.int32)
    alike = (owner_col == owner_row) & ((r256 & 3) == (c256 & 3))
    rank_row = jnp.sum(jnp.where(alike & (r256 < c256), 1, 0), axis=0, keepdims=True)
    rank_col = jnp.sum(jnp.where(alike & (c256 < r256), 1, 0), axis=1, keepdims=True)
    lane_row = iota((1, DR), 1)
    lane_col = iota((DR, 1), 0)
    target_row = owner_row * SLOTS + rank_row * 4 + (lane_row & 3)
    target_col = owner_col * SLOTS + rank_col * 4 + (lane_col & 3)
    n_slots = NDP * SLOTS

    below, above, opposite = block_of(NY - 1), block_of(1), block_of(2)
    up_a.wait_recv()
    up_fa = block(below, A, up)
    dn_b.wait_recv()
    dn_fb = block(above, B, dn)
    relays = [block(below, A, core), block(above, B, core)]
    up_b.wait_recv()
    relays.append(block(below, B, core))
    dn_a.wait_recv()
    relays.append(block(above, A, core))

    l_q.wait()
    l_kv.wait()

    def project(k, first=False):
        add_q = nn(dg[k], qw[k])
        add_kv = nn(dg[k], kvw[k // 2, pl.ds(pl.multiple_of(k % 2 * D, D), D)])
        if first:
            acc[:, : GROUP * HEAD] = add_q
            acc[:, GROUP * HEAD :] = add_kv
        else:
            acc[:, : GROUP * HEAD] += add_q
            acc[:, GROUP * HEAD :] += add_kv

    project(t, True)

    ps_copy.wait_recv()
    l_wt.wait()

    def partial(j, row, rows):
        return nn(ps[0, row : row + rows], wt[j, :D]) + nn(ps[1, row : row + rows], wt[j, D:])

    def rp(n, dev):
        return send(rp_send.at[n], rp_recv.at[n], dev)

    def slot_ready(slot):
        for copy in spread[slot]:
            copy.wait_recv()

    slot_ready(2)
    rp_send[0] = partial(2, 0, HALF).astype(BF16)
    rp0 = rp(0, dn)
    rp_send[1] = partial(2, HALF, HALF).astype(BF16)
    rp1 = rp(1, up)
    project(below)
    project(above)

    up_fa.wait_recv()
    relays.append(block(opposite, A, core))
    dn_fb.wait_recv()
    relays.append(block(opposite, B, core))

    slot_ready(1)
    rp_send[2] = partial(1, 0, HALF).astype(BF16)
    rp2 = rp(2, up)
    slot_ready(3)
    rp_send[3] = partial(3, HALF, HALF).astype(BF16)
    rp3 = rp(3, dn)

    project(opposite)
    g_core.wait_recv()
    project(block_of(0) + oc - c)
    for copy in relays:
        copy.wait_recv()
    for j in range(1, NY):
        project(block_of(j) + oc - c)

    for copy in sq:
        copy.wait_recv()
    total = sg[0]
    for k in range(1, NT):
        total = total + sg[k]
    factor = lax.rsqrt(total / MODEL_WIDTH + EPSILON)
    for i in range((PR + DR) // 128):
        rcol[i * 128 : (i + 1) * 128] = jnp.broadcast_to(factor[i : i + 1], (128, 128)).T

    scale = rcol[PR : PR + DR]
    for i in range(WIDTH // 128):
        pj[:, i * 128 : (i + 1) * 128] = (acc[:, i * 128 : (i + 1) * 128] * scale).astype(BF16)
    for i in range(4):
        rows = iota((n_slots // 4, DR), 0) + i * (n_slots // 4)
        pick = jnp.where(rows == target_row, 1.0, 0.0).astype(BF16)
        placed = nn(pick, pj[:, : GROUP * HEAD]).astype(BF16)
        qo[i * 8 : (i + 1) * 8] = placed.reshape(8, SLOTS, GROUP * HEAD)
    qr[d] = qo[d]
    send_many(qo, qr, QX, True)

    part = partial(3, 0, HALF)
    rp0.wait_recv()
    rp_send[4] = (part + rp_recv[0].astype(F32)).astype(BF16)
    rp4 = rp(4, dn)
    part = partial(1, HALF, HALF)
    rp1.wait_recv()
    rp_send[5] = (part + rp_recv[1].astype(F32)).astype(BF16)
    rp5 = rp(5, up)
    own_sum[:HALF] = partial(0, 0, HALF)
    own_sum[HALF:] = partial(0, HALF, HALF)

    wo_copies = []
    for b in range(NY):
        cols = pl.ds(pl.multiple_of((2 * b + oc) * D, 128), D)
        wo_copies.append(send(wo_hbm.at[:, cols], wob.at[1, b], core))

    root = float(HEAD) ** -0.5
    rows3 = GROUP * 128

    def heads_down(value):
        return jnp.concatenate([value[:, h * HEAD : (h + 1) * HEAD] for h in range(GROUP)], axis=0)

    def heads_across(value):
        return jnp.concatenate([value[h * 128 : (h + 1) * 128] for h in range(GROUP)], axis=1)

    for i in range(2):
        rows = pj[i * 128 : (i + 1) * 128]
        r, cc = iota((rows3, 128), 0) & 127, iota((rows3, 128), 1)
        usable = ((r >> 2) == (cc >> 2)) & ((cc & 3) <= (r & 3))
        query = heads_down(rows)
        own = nt(query, rows[:, GROUP * HEAD : GROUP * HEAD + HEAD]) * root
        own = jnp.where(usable, own, HUGE_NEGATIVE)
        own_top = jnp.max(own, axis=1, keepdims=True)
        own_weights = jnp.where(usable, jnp.exp(own - own_top), 0.0)
        own_mass = jnp.sum(own_weights, axis=1, keepdims=True)
        mine_ref[i, 0] = nn(own_weights.astype(BF16), rows[:, GROUP * HEAD + HEAD :])
        mine_ref[i, 1] = jnp.broadcast_to(own_top, (rows3, 128))
        mine_ref[i, 2] = jnp.broadcast_to(own_mass, (rows3, 128))

    l_lengths.wait()
    wait_many(ids, IDS)
    which = jnp.concatenate([ids[s] for s in range(NDP)], axis=0)
    local = which - (PROMPTS * d).astype(F32)
    match = (local >= 0.0) & (local < float(PROMPTS))
    before = jnp.where(iota((128, 128), 0) < iota((128, 128), 1), 1.0, 0.0).astype(BF16)
    rank = nn(jnp.where(match, 1.0, 0.0).astype(BF16), before)
    lane = iota((NDP, 128), 1)
    table = jnp.zeros((NDP, 128), F32)
    for k in range(4):
        at_k = jnp.sum(
            jnp.where(match & (rank == float(k)), local, 0.0), axis=1, keepdims=True
        )
        table = jnp.where(lane == k, at_k, table)
    table = table.astype(BF16)
    for i in range(4):
        sub = iota((128, NDP), 0)
        spread = jnp.where((sub >> 4) + 8 * i == iota((128, NDP), 1), 1.0, 0.0).astype(BF16)
        wide = nn(spread, table)
        mine = iota((128, 128), 1) == ((iota((128, 128), 0) >> 2) & 3)
        pid = jnp.sum(jnp.where(mine, wide, 0.0), axis=1, keepdims=True)
        pid_ref[i * 128 : (i + 1) * 128] = jnp.broadcast_to(pid, (128, 128))
        lens = jnp.zeros((128, 1), F32)
        for p in range(PROMPTS):
            lens = jnp.where(pid == float(p), lengths_ref[PROMPTS * d + p].astype(F32), lens)
        len_ref[i * 128 : (i + 1) * 128] = jnp.broadcast_to(lens, (128, 128))

    rp2.wait_recv()
    rp4.wait_recv()

    def finish_rows(base, one_slot, two_slot):
        def one(i, carry):
            at = pl.ds(pl.multiple_of(i * 128, 128), 128)
            there = pl.ds(pl.multiple_of(base + i * 128, 128), 128)
            value = own_sum[there] + rp_recv[one_slot, at].astype(F32) + rp_recv[two_slot, at].astype(F32)
            factor = rcol[there]
            kt[base // 128 + i] = (value[:, :HEAD] * factor).astype(BF16).T
            vc[there] = (value[:, HEAD:] * factor).astype(BF16)
            return carry

        lax.fori_loop(0, HALF // 128, one, 0)

    finish_rows(0, 2, 4)
    rp3.wait_recv()
    rp5.wait_recv()
    finish_rows(HALF, 3, 5)

    wait_many(qr, QX)
    def thrice(value):
        return jnp.concatenate([value] * GROUP, axis=0)

    def attend(step, carry):
        away = 4 - step
        planes = [(z + away) % NZ, (z + NZ - away - 4 * (away // 4)) % NZ]
        four = [pl.ds(pl.multiple_of(plane * NX, NX), NX) for plane in planes]
        at = [pl.ds(pl.multiple_of(plane * 64, 64), 64) for plane in planes]

        def both(ref):
            return jnp.concatenate([ref[rows, 0:1] for rows in at], axis=0)

        query = jnp.concatenate([qr[s].reshape(64, GROUP * HEAD) for s in four], axis=0)
        query = heads_down(query)
        pid = thrice(both(pid_ref))
        lens = thrice(both(len_ref))
        live = iota((rows3, LP), 1).astype(F32) < lens
        scores = None
        for p in range(PROMPTS):
            keys = jnp.concatenate([kt[2 * p], kt[2 * p + 1]], axis=1)
            found = nn(query, keys)
            scores = found if p == 0 else jnp.where(pid == float(p), found, scores)
        scores = jnp.where(live, scores * root, HUGE_NEGATIVE)
        top = jnp.max(scores, axis=1, keepdims=True)
        weights = jnp.where(live, jnp.exp(scores - top), 0.0)
        mass = jnp.sum(weights, axis=1, keepdims=True)
        blended = jnp.zeros((rows3, HEAD), F32)
        for p in range(PROMPTS):
            masked = jnp.where(pid == float(p), weights, 0.0).astype(BF16)
            blended = blended + nn(masked, vc[p * LP : (p + 1) * LP])
        result = heads_across((blended / mass).astype(BF16))
        for n in range(2):
            ro_[four[n]] = result[n * 64 : (n + 1) * 64].reshape(NX, SLOTS, GROUP * HEAD)
        level = top + jnp.log(mass)
        row, lane = iota((128, 128), 0), iota((128, 128), 1)
        wide = jnp.zeros((128, 128), F32)
        for h in range(GROUP):
            wide = jnp.where((lane >> 4) == h, level[h * 128 : (h + 1) * 128], wide)
        wide = jnp.where((lane & 15) == (row & 15), wide, 0.0)
        gather = jnp.where((iota((8, 128), 1) >> 4) == iota((8, 128), 0), 1.0, 0.0)
        levels = exact(gather, wide)
        for k in range(8):
            lo[planes[k // 4] * NX + k % 4] = levels[k : k + 1]

        def give(k, carry):
            to = ((z + away) * (1 - k % 2) + (z + NZ - away - 4 * (away // 4)) * (k % 2)) % NZ * NX + k // 2

            @pl.when(to != d)
            def _():
                remote(ro_.at[to], rr.at[d], RX, (to, t)).start()
                remote(lo.at[to], lr.at[d], LX, (to, t)).start()

            return carry

        lax.fori_loop(0, 8, give, 0)
        return carry

    lax.fori_loop(0, 4, attend, 0)
    rr[d] = ro_[d]
    lr[d] = lo[d]
    for i in range(2):
        rows = pl.ds(i * 128, 128)
        target = target_col[i * 128 : (i + 1) * 128]
        take_ref[rows] = jnp.where(iota((128, n_slots), 1) == target, 1.0, 0.0).astype(BF16)
    for copy in l_wo:
        copy.wait()
    for copy in wo_copies:
        copy.wait_recv()
    wait_many(lr, LX)
    levels = jnp.concatenate([lr[s] for s in range(NDP)], axis=0)
    for i in range(2):
        target = target_col[i * 128 : (i + 1) * 128]
        owner = jnp.where(iota((128, NDP), 1) == (target >> 4), 1.0, 0.0)
        level = exact(owner, levels)
        lane = iota((128, 128), 1)
        level = jnp.concatenate(
            [
                jnp.sum(jnp.where(lane == h * 16 + (target & 15), level, 0.0), axis=1, keepdims=True)
                for h in range(GROUP)
            ],
            axis=0,
        )
        own_blended, own_top, own_mass = mine_ref[i, 0], mine_ref[i, 1], mine_ref[i, 2]
        highest = jnp.maximum(level, own_top)
        one, two = jnp.exp(level - highest), jnp.exp(own_top - highest)
        whole = one + own_mass * two
        mine_ref[i, 0] = own_blended * (two / whole)
        mine_ref[i, 1] = one / whole

    wait_many(rr, RX)
    prefix = rr[...].reshape(n_slots, GROUP * HEAD)
    ax_copies = []
    for i in range(2):
        found = heads_down(nn(take_ref[i * 128 : (i + 1) * 128], prefix))
        merged = found * mine_ref[i, 1] + mine_ref[i, 0]
        ax[c, i * 128 : (i + 1) * 128] = heads_across(merged.astype(BF16))
        ax_copies.append(same(ax.at[c, pl.ds(i * 128, 128)], core))

    def out_partial(j, row):
        b = (y + j) % NY
        at = pl.ds(row, DHALF)
        return nn(ax[c, at], wob[0, b]) + nn(ax[oc, at], wob[1, b])

    def out_send(n, j, row, extra, dev):
        value = out_partial(j, row)
        if extra is not None:
            value = value + rs_recv[extra].astype(F32)
        rs_send[n] = value.astype(BF16)
        return send(rs_send.at[n], rs_recv.at[n], dev)

    ax_copies[0].wait_recv()
    o0 = out_send(0, 2, 0, None, dn)
    ax_copies[1].wait_recv()
    o1 = out_send(1, 2, DHALF, None, up)
    o2 = out_send(2, 1, 0, None, up)
    o3 = out_send(3, 3, DHALF, None, dn)
    o0.wait_recv()
    o4 = out_send(4, 3, 0, 0, dn)
    o1.wait_recv()
    o5 = out_send(5, 1, DHALF, 1, up)
    own_a = out_partial(0, 0)
    o2.wait_recv()
    o4.wait_recv()
    own_a = own_a + rs_recv[2].astype(F32) + rs_recv[4].astype(F32)
    out_ref[: DHALF // 4] = own_a.reshape(DHALF // 4, 4, D).astype(BF16)
    first, second = pl.ds(0, DHALF // 4), pl.ds(DHALF // 4, DHALF // 4)
    out_a = local_copy(out_ref.at[first], out_hbm.at[first], 13)
    own_b = out_partial(0, DHALF)
    o3.wait_recv()
    o5.wait_recv()
    own_b = own_b + rs_recv[3].astype(F32) + rs_recv[5].astype(F32)
    out_ref[DHALF // 4 :] = own_b.reshape(DHALF // 4, 4, D).astype(BF16)
    out_b = local_copy(out_ref.at[second], out_hbm.at[second], 14)

    out_a.wait()
    out_b.wait()
    for copy in sent:
        copy.wait_send()
    for ref, n in ((ids, IDS), (qo, QX), (ro_, RX), (lo, LX)):
        many(ref, ss.at[n]).wait()


def shards(
    prompt_states, prompt_lengths, decode_states, sample_owner, sample_local,
    norm_gain, kv_weight, q_weight, output_weight,
):
    hbm = pl.BlockSpec(memory_space=pl.ANY)
    out = pl.pallas_call(
        kernel,
        out_shape=jax.ShapeDtypeStruct((DR // 4, 4, D), BF16),
        in_specs=[hbm] * 9,
        out_specs=hbm,
        scratch_shapes=[
            pltpu.VMEM((D,), F32),
            pltpu.VMEM((1, 64), jnp.int32),
            pltpu.VMEM((1, 64), jnp.int32),
            pltpu.SMEM((NDP * PROMPTS,), jnp.int32),
            pltpu.VMEM((DR // 4, 4, D), BF16),
            pltpu.VMEM((DR // 4, 4, D), BF16),
            pltpu.VMEM((PR, D), BF16),
            pltpu.VMEM((NT, DR, D), BF16),
            pltpu.VMEM((NC, PR, D), BF16),
            pltpu.VMEM((NT, 16, 128), F32),
            pltpu.VMEM((NDP, 1, 128), F32),
            pltpu.VMEM((NT, D, GROUP * HEAD), BF16),
            pltpu.VMEM((NY, 2 * D, 2 * HEAD), BF16),
            pltpu.VMEM((NY, 2 * D, 2 * HEAD), BF16),
            pltpu.VMEM((NC, NY, GROUP * HEAD, D), BF16),
            pltpu.VMEM((6, HALF, 2 * HEAD), BF16),
            pltpu.VMEM((6, HALF, 2 * HEAD), BF16),
            pltpu.VMEM((PR, 2 * HEAD), F32),
            pltpu.VMEM((PR // 128, HEAD, 128), BF16),
            pltpu.VMEM((PR, HEAD), BF16),
            pltpu.VMEM((DR, WIDTH), F32),
            pltpu.VMEM((DR, WIDTH), BF16),
            pltpu.VMEM((NDP, SLOTS, GROUP * HEAD), BF16),
            pltpu.VMEM((NDP, SLOTS, GROUP * HEAD), BF16),
            pltpu.VMEM((NDP, 1, 128), F32),
            pltpu.VMEM((NDP, 1, 128), F32),
            pltpu.VMEM((2, 3, GROUP * 128, 128), F32),
            pltpu.VMEM((DR, NDP * SLOTS), BF16),
            pltpu.VMEM((NDP, SLOTS, GROUP * HEAD), BF16),
            pltpu.VMEM((NDP, SLOTS, GROUP * HEAD), BF16),
            pltpu.VMEM((NC, DR, GROUP * HEAD), BF16),
            pltpu.VMEM((6, DHALF, D), BF16),
            pltpu.VMEM((6, DHALF, D), BF16),
            pltpu.VMEM((NDP * SLOTS, 128), F32),
            pltpu.VMEM((NDP * SLOTS, 128), F32),
            pltpu.VMEM((PR + DR, 128), F32),
            pltpu.SemaphoreType.DMA((N_SEM,)),
            pltpu.SemaphoreType.DMA((N_SEM,)),
            pltpu.SemaphoreType.DMA((15,)),
        ],
        compiler_params=pltpu.CompilerParams(
            collective_id=0, has_side_effects=True, vmem_limit_bytes=56 * 1024 * 1024
        ),
    )(
        decode_states,
        prompt_states.reshape(PR, D),
        norm_gain,
        sample_owner.reshape(1, 64),
        sample_local.reshape(1, 64),
        prompt_lengths,
        kv_weight.reshape(NY, 2 * D, 2 * HEAD),
        q_weight.reshape(NT, D, GROUP * HEAD),
        output_weight.reshape(GROUP * HEAD, MODEL_WIDTH),
    )
    return out


def solution(mesh):
    placed = (
        P("dp", None, "tensor"),
        P(),
        P("dp", None, "tensor"),
        P("dp", None),
        P("dp"),
        P("tensor"),
        P(None, "tensor", None),
        P(None, "tensor", None),
        P("tensor", None, None),
    )
    return jax.shard_map(
        shards, mesh=mesh, in_specs=placed, out_specs=P("dp", None, "tensor"), check_vma=False
    )
```
